256 devices in a mesh: ctx: 32 (over z, y), head: 8 (over x, core).
Axes of the slice: x: 4, y: 4, z: 8, core: 2. Of those that a mesh axis runs over, the one named last changes fastest.
Arguments:
- query: bfloat16 [8192, 4096], P('ctx', 'head'), may hold values from -6 to 6
- key: bfloat16 [8192, 4096], P('ctx', 'head'), may hold values from -6 to 6
- value: bfloat16 [8192, 4096], P('ctx', 'head'), may hold values from -6 to 6
- episode_lengths: int32 [8], replicated, may hold values from 1 to 4096, 8192 in all
- attn_gain: float32 [4096], P('head'), may hold values from 0.1 to 1.9
- out_weight: bfloat16 [4096, 3072], P('head', 'ctx'), may hold values from -0.09375 to 0.09375
- residual: bfloat16 [8192, 3072], P('ctx', 'head'), may hold values from -36 to 36
- norm_gain: float32 [3072], P('head'), may hold values from 0.1 to 1.9
- expert_ids: int32 [8192, 2], P('ctx'), may hold values from 0 to 31, all different within a row; in each aligned block of 256 rows (0 to 255, 256 to 511, ...) at most 24 rows name the same one
- route_weights: int32 [8192, 2], P('ctx'), may hold values from 4096 to 65535
- gate_weight: bfloat16 [32, 3072, 5120], P('ctx', None, 'head'), may hold values from -0.109375 to 0.109375
- up_weight: bfloat16 [32, 3072, 5120], P('ctx', None, 'head'), may hold values from -0.109375 to 0.109375
- down_weight: bfloat16 [32, 5120, 3072], P('ctx', 'head'), may hold values from -0.125 to 0.125
Outputs:
- layer_out: bfloat16 [8192, 3072], P('ctx', 'head')
The draws below stay inside these ranges and needn't reach their ends.
Inputs may be any that keep to these rules, and one draw needn't show every extreme that they name: `expert_ids`: in the rows of one device (256 tokens) no expert is named by more than 24 rows, a bound that some block reaches; a row names two different experts.
All inputs are finite; a program needn't handle non-finite values.
Results may differ from the reference program's by a relative error of at most 0.012.
Values may be sent and summed in bfloat16 or wider, within the bound.
No kernel may reach another device: no remote copies, remote signals or barrier semaphores. Data moves between devices by JAX's collectives and lax.ppermute only.
A program may use at most 128 MiB of HBM per device.

```python
import math
import jax
import jax.numpy as jnp
import numpy as np
from jax import lax

D = 3072
HEADS = 32
HEAD_DIM = 128
FF = 5120
TOK_DEV = 256
EPISODES = 8
HQ = 4096
EXPERTS = 32
TOKENS = 8192
CAP = 24
N_HEAD = 8


def draw_residual(key, part):
    first, second, third = jax.random.split(key, 3)
    base = jnp.clip(jax.random.normal(first, (TOKENS, D), jnp.float32), -4.0, 4.0)
    rows = jnp.exp(jax.random.uniform(second, (TOKENS, 1), jnp.float32, math.log(0.3), math.log(3.0)))
    columns = jnp.exp(jax.random.uniform(third, (1, D), jnp.float32, math.log(0.3), math.log(3.0)))
    return (base * rows * columns).astype(jnp.bfloat16)


def set_ends(entries, own_key, least, top_value):
    index_at = [jax.random.randint(jax.random.fold_in(own_key, axis), (), 0, length) for axis, length in enumerate(entries.shape)]
    main_axis = entries.shape.index(max(entries.shape))
    neighbour = index_at[:main_axis] + [(index_at[main_axis] + 1) % entries.shape[main_axis]] + index_at[main_axis + 1:]
    return entries.at[tuple(index_at)].set(least).at[tuple(neighbour)].set(top_value)


def with_spikes(result, key, source, target, parts, factor):
    owner, partner = [(jnp.arange(result.shape[axis_at]) // (result.shape[axis_at] // parts)).reshape([-1 if axis == axis_at else 1 for axis in range(result.ndim)]) for axis_at in (source, target)]
    chosen = jax.random.permutation(key, parts)[partner]
    strong = (owner == chosen) | (owner == (partner + parts // 2) % parts)
    return jnp.where(strong, factor * result, result)


def shard_levels(own_key, dims, pieces, low, high):
    level, own = 1.0, jax.random.fold_in(own_key, 6)
    for position, blocks in pieces:
        draws = jnp.exp(jax.random.uniform(jax.random.fold_in(own, position), (blocks,), jnp.float32, low / len(pieces), high / len(pieces)))
        level = level * jnp.repeat(draws, dims[position] // blocks).reshape([-1 if axis == position else 1 for axis in range(len(dims))])
    return level


def length_profile(amount, total, bound, skew):
    portions = [(1 << 20) // math.isqrt(rank ** skew) + 1 for rank in range(2, amount + 1)]
    rest, counts = total - bound - (amount - 1), [1] * (amount - 1)
    while rest > 0:
        candidates = [i for i in range(amount - 1) if counts[i] < bound]
        pool, remaining = sum([portions[i] for i in candidates]), rest
        for i in candidates:
            extra = min(bound - counts[i], max(1, remaining * portions[i] // pool), rest)
            counts[i] = counts[i] + extra
            rest = rest - extra
    return np.array([bound] + counts)


def uneven_parts(key, amount, total, most, lean):
    if amount == 2:
        one = jax.random.randint(key, (), max(1, total - most), min(most, total - 1) + 1)
        return jnp.stack([one, total - one])
    sizes = jnp.asarray(length_profile(amount, total, most, lean), jnp.int32)
    pairs = (amount - 1) // 2
    giver, taker = sizes[1:1 + 2 * pairs:2], sizes[2:2 + 2 * pairs:2]
    slack = jnp.minimum(giver - 1, most - taker)
    passed = jax.random.randint(jax.random.fold_in(key, 1), (pairs,), 0, 1 << 20) % (slack + 1)
    sizes = sizes.at[1:1 + 2 * pairs:2].set(giver - passed).at[2:2 + 2 * pairs:2].set(taker + passed)
    return sizes[jax.random.permutation(jax.random.fold_in(key, 2), amount)]


def routed_block(own_key, own, number, rows, number_of, top, limit, slope):
    sequence = jax.random.permutation(own_key, number_of)
    packed, ordinary = load_shares(number_of, rows * top, limit, slope, True), load_shares(number_of, rows * top, limit, slope, False)
    places = jnp.arange(number_of)

    def named(sizes, turn):
        used = int((sizes > 0).sum())
        fixed = max(1, used // 4)
        moved = fixed + (places - fixed + turn * (used - fixed)) % max(1, number_of - fixed)
        return jnp.zeros((number_of,), jnp.int32).at[sequence[jnp.where(places < fixed, places, moved)]].set(jnp.asarray(sizes, jnp.int32))

    sizes = jnp.where(number % 4 == 0, named(packed, number // 4), named(ordinary, number - number // 4 - 1))
    mixed = jax.random.permutation(jax.random.fold_in(own, 3), number_of)
    donor, taker = mixed[0:number_of // 2 * 2:2], mixed[1:number_of // 2 * 2:2]
    slack = jnp.minimum(sizes[donor] - 1, limit - sizes[taker]) // 2
    slack = jnp.where((donor == sequence[0]) | (taker == sequence[0]) | (sizes[taker] == 0), 0, jnp.maximum(slack, 0))
    moved = jax.random.randint(jax.random.fold_in(own, 4), (number_of // 2,), 0, 1 << 20) % (slack + 1)
    sizes = sizes.at[donor].add(-moved).at[taker].add(moved)
    labels = jnp.searchsorted(jnp.cumsum(sizes), jnp.arange(rows * top), side="right").astype(jnp.int32)
    listing = labels.reshape(top, rows).T
    listing = listing[jax.random.permutation(jax.random.fold_in(own, 1), rows)]
    turn = jax.random.randint(jax.random.fold_in(own, 2), (rows, 1), 0, top)
    return jnp.take_along_axis(listing, (jnp.arange(top)[None, :] + turn) % top, axis=1)


def load_shares(count, total, bound, slope, full):
    loads = [(1 << 20) // math.isqrt(rank ** slope) + 1 for rank in range(1, count + 1)]
    largest = bound if full else min(bound, max(-(-total // count), total * loads[0] // sum(loads)))
    least = 1 if total - largest >= count - 1 else 0
    holding, spare = [largest] + [least] * (count - 1), total - largest - least * (count - 1)
    while spare > 0:
        candidates = [i for i in range(1, count) if holding[i] < largest] or [i for i in range(1, count) if holding[i] < bound]
        pool, budget = sum([loads[i] for i in candidates]), spare
        for i in candidates:
            extra = min(bound - holding[i], max(1, budget * loads[i] // pool), spare)
            holding[i] = holding[i] + extra
            spare = spare - extra
    return np.array(holding)


def normal_values(rng, dims, spread, limit, pieces=(), held_as=jnp.bfloat16):
    entries = jax.random.normal(rng, dims, jnp.float32) * spread
    if len(pieces) > 0:
        entries = shard_levels(rng, dims, pieces, -0.22, 0.18) * entries
    return jnp.clip(entries, min=-limit, max=limit).astype(held_as)


def noise_with(rng, dims, spread, limit, pieces, heavy, kind=jnp.bfloat16):
    values = spread * jax.random.normal(rng, dims, jnp.float32)
    if pieces:
        values = values * shard_levels(rng, dims, pieces, -0.22, 0.18)
    return jnp.clip(with_spikes(values, jax.random.fold_in(rng, 3), *heavy), -limit, limit).astype(kind)


def setup_inputs(seed: int = 0) -> dict:
    splits = jax.random.split(jax.random.key(seed), 14)
    query = normal_values(splits[0], (TOKENS, HQ), 1.0, 6.0, ((0, 32), (1, 8)))
    key = normal_values(splits[1], (TOKENS, HQ), 1.0, 6.0, ((0, 32), (1, 8)))
    value = normal_values(splits[2], (TOKENS, HQ), 1.0, 6.0, ((0, 32), (1, 8)))
    episode_lengths = uneven_parts(splits[3], EPISODES, TOKENS, TOKENS // 2, 2).astype(jnp.int32)
    attn_gain = jnp.clip(1.0 + 0.18 * jax.random.normal(splits[4], (HQ,), jnp.float32), 0.1, 1.9)
    out_weight = normal_values(splits[5], (HQ, D), HQ ** -0.5, 0.09375, ((0, 8), (1, 32)))
    residual = draw_residual(jax.random.fold_in(splits[13], 71), 0)
    norm_gain = jnp.clip(1.0 + 0.18 * jax.random.normal(splits[7], (D,), jnp.float32), 0.1, 1.9)
    expert_ids_keys = jax.random.split(jax.random.fold_in(splits[8], 1), TOKENS // TOK_DEV)
    expert_ids_turns = jax.random.permutation(jax.random.fold_in(splits[8], 3), TOKENS // TOK_DEV)
    expert_ids = jax.vmap(lambda own, number: routed_block(jax.random.fold_in(splits[8], 2), own, number, TOK_DEV, EXPERTS, 2, CAP, 2))(expert_ids_keys, expert_ids_turns).reshape((TOKENS, 2))
    route_weights = set_ends(jax.random.randint(splits[9], (TOKENS, 2), 4096, 65536), jax.random.fold_in(splits[9], 1), 4096, 65535).astype(jnp.int32)
    gate_weight = normal_values(splits[10], (EXPERTS, D, FF), D ** -0.5, 0.109375, ((0, 32), (2, 8)))
    up_weight = normal_values(splits[11], (EXPERTS, D, FF), D ** -0.5, 0.109375, ((0, 32), (2, 8)))
    down_weight = noise_with(splits[12], (EXPERTS, FF, D), FF ** -0.5, 0.125, ((0, 32), (1, 8)), (1, 2, 8, 2.0))
    return dict(query=query, key=key, value=value, episode_lengths=episode_lengths, attn_gain=attn_gain, out_weight=out_weight, residual=residual, norm_gain=norm_gain, expert_ids=expert_ids, route_weights=route_weights, gate_weight=gate_weight, up_weight=up_weight, down_weight=down_weight)


def episode_of(positions, lengths):
    starts = (jnp.cumsum(lengths) - lengths).astype(jnp.int32)
    return (lax.optimization_barrier(jnp.sum((starts[None, :] <= positions[:, None]).astype(jnp.int32), axis=1)) - 1).astype(jnp.int32)

def attention(query, key, value, episode_lengths, attn_gain):
    total = query.shape[0]
    blocks = total // TOK_DEV
    positions = jnp.arange(total, dtype=jnp.int32)
    episode = episode_of(positions, episode_lengths)
    lifted_query = jax.nn.silu(query.astype(jnp.float32)).reshape(blocks, TOK_DEV, HEADS, HEAD_DIM)
    lifted_key = jax.nn.silu(key.astype(jnp.float32)).reshape(blocks, TOK_DEV, HEADS, HEAD_DIM)
    value_rows = value.astype(jnp.float32).reshape(blocks, TOK_DEV, HEADS, HEAD_DIM)
    episode_blocks = episode.reshape(blocks, TOK_DEV)
    order = jnp.arange(TOK_DEV, dtype=jnp.int32)
    causal = order[:, None] >= order[None, :]
    highest = lax.Precision.HIGHEST

    def advance(carry, inputs):
        state, prior = carry
        block_query, block_key, block_value, block_episode = inputs
        allowed = (causal & (block_episode[:, None] == block_episode[None, :])).astype(jnp.float32)
        scores = jnp.einsum('thd,shd->hts', block_query, block_key, precision=highest)
        inside = jnp.einsum('hts,shd->thd', scores * allowed[None], block_value, precision=highest)
        carry_mask = (block_episode == prior).astype(jnp.float32)
        outside = jnp.einsum('thd,hde->the', block_query, state, precision=highest)
        final = block_episode[-1].astype(jnp.int32)
        keep = (block_episode == final).astype(jnp.float32)
        fresh = jnp.einsum('shd,she->hde', block_key * keep[:, None, None], block_value, precision=highest)
        state = jnp.where(final == prior, state + fresh, fresh)
        return ((state, final), inside + outside * carry_mask[:, None, None])
    start_state = (jnp.zeros((HEADS, HEAD_DIM, HEAD_DIM), jnp.float32), jnp.array(-1, jnp.int32))
    _, outputs = lax.scan(advance, start_state, (lifted_query, lifted_key, value_rows, episode_blocks))
    attn = outputs.reshape(total, HEADS, HEAD_DIM)
    mean_square = lax.optimization_barrier(jnp.mean(attn * attn, axis=2, keepdims=True))
    scaled = attn * lax.rsqrt(mean_square + 1e-06) * attn_gain.reshape(HEADS, HEAD_DIM)
    return scaled.reshape(total, HQ).astype(jnp.bfloat16)

def reference(query, key, value, episode_lengths, attn_gain, out_weight, residual, norm_gain, expert_ids, route_weights, gate_weight, up_weight, down_weight):
    headed = attention(query, key, value, episode_lengths, attn_gain)
    mixed = jnp.dot(headed, out_weight, preferred_element_type=jnp.float32)
    hidden_state = residual.astype(jnp.float32) + mixed
    mean_square = lax.optimization_barrier(jnp.mean(hidden_state * hidden_state, axis=1, keepdims=True))
    normed = (hidden_state * lax.rsqrt(mean_square + 1e-06) * norm_gain).astype(jnp.bfloat16)
    raw_weights = route_weights.astype(jnp.float32)
    share = (raw_weights / lax.optimization_barrier(jnp.sum(raw_weights, axis=1, keepdims=True))).reshape(-1)
    flat_ids = expert_ids.reshape(-1)
    pair_rows = jnp.arange(flat_ids.shape[0], dtype=jnp.int32) // 2
    room = EXPERTS * CAP
    slice_width = FF // N_HEAD

    def expert_step(total, inputs):
        expert, gate_one, up_one, down_one = inputs
        matches = flat_ids == expert
        chosen = jnp.nonzero(matches, size=room, fill_value=0)[0].astype(jnp.int32)
        count = jnp.sum(matches.astype(jnp.int32)).astype(jnp.int32)
        valid = (jnp.arange(room, dtype=jnp.int32) < count).astype(jnp.float32)
        rows = normed[pair_rows[chosen]]
        gate = jnp.dot(rows, gate_one, preferred_element_type=jnp.float32)
        up = jnp.dot(rows, up_one, preferred_element_type=jnp.float32)
        gated = (jax.nn.silu(gate) * up).astype(jnp.bfloat16)
        combined = jnp.zeros((room, D), jnp.float32)
        for part_index in range(N_HEAD):
            lower = part_index * slice_width
            upper = lower + slice_width
            partial_value = jnp.dot(gated[:, lower:upper], down_one[lower:upper], preferred_element_type=jnp.float32).astype(jnp.bfloat16)
            combined = combined + partial_value.astype(jnp.float32)
        contribution = combined * (share[chosen] * valid)[:, None]
        total = total.at[pair_rows[chosen]].add(contribution)
        return (total, None)
    experts_list = jnp.arange(EXPERTS, dtype=jnp.int32)
    moe, _ = lax.scan(expert_step, jnp.zeros((TOKENS, D), jnp.float32), (experts_list, gate_weight, up_weight, down_weight))
    return (hidden_state + moe).astype(jnp.bfloat16)
```

```python
import jax
import jax.numpy as jnp
from jax import lax
from jax.sharding import Mesh
from jax.sharding import PartitionSpec as P

HEAD_DIM = 128
CTX = ("ctx_0", "ctx_1")


highest = lax.Precision.HIGHEST


def nothing_yet(value, identity):
    return jax.tree.map(
        lambda a, e: jnp.broadcast_to(jnp.asarray(e, a.dtype), a.shape), value, identity
    )


def prefix_by_axis(value, axes, combine, identity):
    before = start = nothing_yet(value, identity)
    so_far = value
    for axis in reversed(axes):
        length, position = (lax.axis_size(axis), lax.axis_index(axis))
        pieces = jax.tree.map(
            lambda part, kind: lax.all_gather(part.astype(kind), axis),
            so_far,
            (jnp.bfloat16, jnp.bfloat16),
        )
        inside, so_far = (start, start)
        for k in range(length):
            passed = k < position
            so_far = combine(
                so_far, jax.tree.map(lambda part, own: part[k].astype(own.dtype), pieces, value)
            )
            inside = jax.tree.map(lambda new, old: jnp.where(passed, new, old), so_far, inside)
        before = combine(inside, before)
    return before


def whole_of(value, axes, dim):
    for axis in reversed(axes):
        value = lax.all_gather(value, axis, axis=dim, tiled=True)
    return value


def split_up(value, dim, length):
    before, after = (value.shape[:dim], value.shape[dim + 1 :])
    return jnp.moveaxis(value.reshape(*before, length, -1, *after), dim, 0)


def sent_and_summed(value, axis, dim):
    parts = split_up(value, dim, lax.axis_size(axis))
    arrived = lax.all_to_all(parts, axis, split_axis=0, concat_axis=0, tiled=True)
    return arrived.astype(jnp.float32).sum(axis=0)


def sent_to_all(value, axis):
    copies = jnp.broadcast_to(value, (lax.axis_size(axis), *value.shape))
    return lax.all_to_all(copies, axis, split_axis=0, concat_axis=0, tiled=True)


def over_copies(value, axis):
    everything = sent_to_all(value, axis)
    return jnp.sum(everything, axis=0)


def episode_of(positions, lengths):
    count = lengths.shape[0]
    ahead = jnp.arange(count)[:, None] > jnp.arange(count)[None, :]
    starts = jnp.sum(jnp.where(ahead, lengths[None, :], 0), axis=1)
    return jnp.sum((starts[None, :] <= positions[:, None]).astype(jnp.int32), axis=1) - 1


def link_states(earlier, latter):
    marker = jnp.maximum(earlier[0], latter[0])
    joined = jnp.where(latter[0][0] > 0.0, latter[1], earlier[1] + latter[1])
    return (marker, joined)


def on_device(
    query,
    key,
    value,
    episode_lengths,
    attn_gain,
    out_weight,
    residual,
    norm_gain,
    expert_ids,
    route_weights,
    gate_weight,
    up_weight,
    down_weight,
):
    tok_rows = query.shape[0]
    head_size = HEAD_DIM
    heads_local = query.shape[1] // head_size
    own_index = lax.axis_index(CTX)
    ctx_count = lax.axis_size(CTX)
    positions = own_index * tok_rows + jnp.arange(tok_rows, dtype=jnp.int32)
    episode = episode_of(positions, episode_lengths)
    prior = episode_of(positions[:1] - 1, episode_lengths)[0]
    final = episode[-1]
    lifted_query = jax.nn.silu(query.astype(jnp.float32)).reshape(tok_rows, heads_local, head_size)
    lifted_key = jax.nn.silu(key.astype(jnp.float32)).reshape(tok_rows, heads_local, head_size)
    value_rows = value.astype(jnp.float32).reshape(tok_rows, heads_local, head_size)
    keep = (episode == final).astype(jnp.float32)
    state = jnp.einsum(
        "shd,she->hde", lifted_key * keep[:, None, None], value_rows, precision=highest
    )
    marker = (final != prior).astype(jnp.float32).reshape(1)
    blank = (jnp.zeros((1,), jnp.float32), jnp.zeros_like(state))
    carried = prefix_by_axis((marker, state), CTX, link_states, blank)
    carry_state = carried[1]
    order = jnp.arange(tok_rows, dtype=jnp.int32)
    allowed = ((order[:, None] >= order[None, :]) & (episode[:, None] == episode[None, :])).astype(
        jnp.float32
    )
    scores = jnp.einsum("thd,shd->hts", lifted_query, lifted_key, precision=highest)
    inside = jnp.einsum("hts,shd->thd", scores * allowed[None], value_rows, precision=highest)
    outside = jnp.einsum("thd,hde->the", lifted_query, carry_state, precision=highest)
    attn = inside + outside * (episode == prior).astype(jnp.float32)[:, None, None]
    mean_square = jnp.mean(attn * attn, axis=2, keepdims=True)
    scaled = attn * lax.rsqrt(mean_square + 1e-06) * attn_gain.reshape(heads_local, head_size)
    headed = scaled.reshape(tok_rows, heads_local * head_size).astype(jnp.bfloat16)
    mixed_part = jnp.dot(headed, whole_of(out_weight, CTX, 1), preferred_element_type=jnp.float32)
    width = mixed_part.shape[1]
    mixed_slice = sent_and_summed(mixed_part.astype(jnp.bfloat16), "head", 1)
    hidden_slice = residual.astype(jnp.float32) + mixed_slice
    squares = over_copies(jnp.sum(hidden_slice * hidden_slice, axis=1), "head")
    normed = (hidden_slice * lax.rsqrt(squares / width + 1e-06)[:, None] * norm_gain).astype(
        jnp.bfloat16
    )
    experts_count = gate_weight.shape[0] * ctx_count
    capacity = 3 * tok_rows // experts_count
    flat_ids = expert_ids.reshape(-1)
    pair_order = jnp.arange(flat_ids.shape[0])
    same = (flat_ids[:, None] == flat_ids[None, :]) & (pair_order[:, None] > pair_order[None, :])
    slot = jnp.sum(same.astype(jnp.int32), axis=1)
    source_rows = jnp.repeat(normed, 2, axis=0)
    outgoing = (
        jnp.zeros((experts_count, capacity, normed.shape[1]), jnp.bfloat16)
        .at[flat_ids, slot]
        .set(source_rows)
    )
    raw_weights = route_weights.astype(jnp.float32)
    share = (raw_weights / jnp.sum(raw_weights, axis=1, keepdims=True)).reshape(-1)
    full_rows = lax.all_gather(
        lax.all_to_all(outgoing, CTX, split_axis=0, concat_axis=0, tiled=True),
        "head",
        axis=2,
        tiled=True,
    )
    flat = full_rows.reshape(-1, full_rows.shape[2])
    gate = jnp.dot(flat, gate_weight[0], preferred_element_type=jnp.float32)
    up = jnp.dot(flat, up_weight[0], preferred_element_type=jnp.float32)
    gated = (jax.nn.silu(gate) * up).astype(jnp.bfloat16)
    partial_value = jnp.dot(gated, down_weight[0], preferred_element_type=jnp.float32).astype(
        jnp.bfloat16
    )
    answer_partial_value = partial_value.reshape(
        full_rows.shape[0], full_rows.shape[1], partial_value.shape[1]
    )
    summed = sent_and_summed(
        lax.optimization_barrier(answer_partial_value).astype(jnp.float32).astype(jnp.bfloat16),
        "head",
        2,
    )
    returned = lax.all_to_all(
        summed.astype(jnp.bfloat16), CTX, split_axis=0, concat_axis=0, tiled=True
    ).astype(summed.dtype)
    picked = returned[flat_ids, slot]
    weighted = jnp.sum((picked * share[:, None]).reshape(tok_rows, 2, picked.shape[1]), axis=1)
    return (hidden_slice + weighted).astype(jnp.bfloat16)


def solution(mesh):
    torus = Mesh(mesh.devices.reshape(8, 4, mesh.shape["head"]), ("ctx_0", "ctx_1", "head"))
    in_specs = (
        P(CTX, "head"),
        P(CTX, "head"),
        P(CTX, "head"),
        P(),
        P("head"),
        P("head", CTX),
        P(CTX, "head"),
        P("head"),
        P(CTX, None),
        P(CTX, None),
        P(CTX, None, "head"),
        P(CTX, None, "head"),
        P(CTX, "head", None),
    )
    out_specs = P(CTX, "head")
    return jax.shard_map(
        on_device, mesh=torus, in_specs=in_specs, out_specs=out_specs, check_vma=False
    )
```

```python
import jax
import jax.numpy as jnp
from jax import lax
from jax.sharding import Mesh
from jax.sharding import PartitionSpec as P

HEAD_DIM = 128
LONGEST = 4096
CTX = ("z", "y")
HEAD = ("x", "core")

highest = lax.Precision.HIGHEST


def shift(value, axis, step):
    size = lax.axis_size(axis)
    return lax.ppermute(value, axis, [(i, (i + step) % size) for i in range(size)])


def put(buffer, block, index):
    return lax.dynamic_update_slice_in_dim(buffer, block[None], index, 0)


def gathered_over_y(block):
    size, me = lax.axis_size("y"), lax.axis_index("y")
    buffer = put(jnp.zeros((size, *block.shape), block.dtype), block, me)
    arrived = [(step, shift(block, "y", step)) for step in (1, -1, 2)]
    for step, part in arrived:
        buffer = put(buffer, part, (me - step) % size)
    return buffer.reshape(-1, block.shape[1])


def gathered_over_z(block):
    size, me = lax.axis_size("z"), lax.axis_index("z")
    buffer = put(jnp.zeros((size, *block.shape), block.dtype), block, me)
    half = block.shape[0] // 2
    up = down = block
    for step in range(1, size // 2):
        up, down = shift(up, "z", 1), shift(down, "z", -1)
        buffer = put(buffer, up, (me - step) % size)
        buffer = put(buffer, down, (me + step) % size)
    last = jnp.concatenate([shift(up[:half], "z", 1), shift(down[half:], "z", -1)])
    return put(buffer, last, (me + size // 2) % size)


def episode_of(positions, lengths):
    count = lengths.shape[0]
    ahead = jnp.arange(count)[:, None] > jnp.arange(count)[None, :]
    starts = jnp.sum(jnp.where(ahead, lengths[None, :], 0), axis=1)
    return jnp.sum((starts[None, :] <= positions[:, None]).astype(jnp.int32), axis=1) - 1


def prior_state(state, last):
    goal = last(1)
    sent = state.astype(jnp.bfloat16)
    total = 0.0
    for step in (1, 2, 3, 4):
        total = total + jnp.where(last(step) == goal, shift(sent, CTX, step).astype(jnp.float32), 0.0)
    for step in (4, 8):
        far = shift(total.astype(jnp.bfloat16), CTX, step).astype(jnp.float32)
        total = total + jnp.where(last(step + 1) == goal, far, 0.0)
    return total


def summed_over_head(part):
    x, core = lax.axis_index("x"), lax.axis_index("core")

    def pair(distance):
        target = (x + distance) % 4
        other = shift(part(target, 1 - core).astype(jnp.bfloat16), "core", 1)
        return part(target, core) + other.astype(jnp.float32)

    far = pair(2).astype(jnp.bfloat16)
    half = far.shape[0] // 2
    above = shift(far[:half], "x", 1)
    below = shift(far[half:], "x", -1)
    up, down = pair(1), pair(3)
    up = jnp.concatenate([up[:half] + above.astype(jnp.float32), up[half:]]).astype(jnp.bfloat16)
    down = jnp.concatenate([down[:half], down[half:] + below.astype(jnp.float32)]).astype(jnp.bfloat16)
    up, down = shift(up, "x", 1), shift(down, "x", -1)
    return pair(0) + up.astype(jnp.float32) + down.astype(jnp.float32)


def blocks_over_head(block):
    x, core = lax.axis_index("x"), lax.axis_index("core")
    half = block.shape[0] // 2

    def both(value, source):
        return [(source * 2 + core, value), (source * 2 + 1 - core, shift(value, "core", 1))]

    found = both(block, x)
    up, down = shift(block, "x", 1), shift(block, "x", -1)
    far = jnp.concatenate([shift(up[:half], "x", 1), shift(down[half:], "x", -1)])
    found += both(up, (x + 3) % 4)
    found += both(down, (x + 1) % 4)
    found += both(far, (x + 2) % 4)
    return found


def dot(a, b):
    return jnp.dot(a, b, preferred_element_type=jnp.float32)


def on_device(
    query,
    key,
    value,
    episode_lengths,
    attn_gain,
    out_weight,
    residual,
    norm_gain,
    expert_ids,
    route_weights,
    gate_weight,
    up_weight,
    down_weight,
):
    tok_rows = query.shape[0]
    heads_local = query.shape[1] // HEAD_DIM
    features = residual.shape[1]
    own_index = lax.axis_index(CTX)
    experts_count = gate_weight.shape[0] * lax.axis_size(CTX)
    capacity = 3 * tok_rows // experts_count
    rows = experts_count * capacity

    whole_weight = gathered_over_z(gathered_over_y(out_weight.T))

    positions = own_index * tok_rows + jnp.arange(tok_rows, dtype=jnp.int32)
    episode = episode_of(positions, episode_lengths)
    lasts = episode_of((own_index + 1 - jnp.arange(LONGEST // tok_rows + 2, dtype=jnp.int32)) * tok_rows - 1, episode_lengths)
    final, prior = lasts[0], lasts[1]
    lifted_query = jax.nn.silu(query.astype(jnp.float32)).reshape(tok_rows, heads_local, HEAD_DIM)
    lifted_key = jax.nn.silu(key.astype(jnp.float32)).reshape(tok_rows, heads_local, HEAD_DIM)
    value_rows = value.astype(jnp.float32).reshape(tok_rows, heads_local, HEAD_DIM)
    keep = (episode == final).astype(jnp.float32)
    state = jnp.einsum("shd,she->hde", lifted_key * keep[:, None, None], value_rows, precision=highest)
    carry_state = prior_state(state, lambda back: lasts[back])
    order = jnp.arange(tok_rows, dtype=jnp.int32)
    allowed = ((order[:, None] >= order[None, :]) & (episode[:, None] == episode[None, :])).astype(
        jnp.float32
    )
    scores = jnp.einsum("thd,shd->hts", lifted_query, lifted_key, precision=highest)
    inside = jnp.einsum("hts,shd->thd", scores * allowed[None], value_rows, precision=highest)
    outside = jnp.einsum("thd,hde->the", lifted_query, carry_state, precision=highest)
    attn = inside + outside * (episode == prior).astype(jnp.float32)[:, None, None]
    mean_square = jnp.mean(attn * attn, axis=2, keepdims=True)
    scaled = attn * lax.rsqrt(mean_square + 1e-06) * attn_gain.reshape(heads_local, HEAD_DIM)
    headed = scaled.reshape(tok_rows, heads_local * HEAD_DIM).astype(jnp.bfloat16)

    def mixed_for(x, core):
        columns = lax.dynamic_index_in_dim(whole_weight, x * 2 + core, 0, keepdims=False)
        return lax.dot_general(headed, columns, (((1,), (1,)), ((), ())), preferred_element_type=jnp.float32)

    hidden = residual.astype(jnp.float32) + summed_over_head(mixed_for)
    scaled_rows = (hidden * norm_gain).astype(jnp.bfloat16)

    flat_ids = expert_ids.reshape(-1)
    pair_order = jnp.arange(flat_ids.shape[0])
    same = (flat_ids[:, None] == flat_ids[None, :]) & (pair_order[:, None] > pair_order[None, :])
    slot = jnp.sum(same.astype(jnp.int32), axis=1)
    place = (flat_ids * capacity + slot).reshape(tok_rows, 2)
    row_order = jnp.arange(rows, dtype=jnp.int32)
    chosen = (row_order[:, None] == place[:, 0][None, :]) | (row_order[:, None] == place[:, 1][None, :])
    outgoing = dot(chosen.astype(jnp.bfloat16), scaled_rows).astype(jnp.bfloat16)
    arrived = lax.all_to_all(
        outgoing.reshape(experts_count, capacity, features), CTX, split_axis=0, concat_axis=0, tiled=True
    ).reshape(rows, features)

    gains = blocks_over_head(1.0 / (norm_gain * norm_gain))
    gate = up = squares = 0.0
    for (source, block), (_, inverse) in zip(blocks_over_head(arrived), gains):
        wide = block.astype(jnp.float32)
        squares = squares + jnp.sum(wide * wide * inverse, axis=1, keepdims=True)
        start = source * features
        gate = gate + dot(block, lax.dynamic_slice_in_dim(gate_weight[0], start, features, 0))
        up = up + dot(block, lax.dynamic_slice_in_dim(up_weight[0], start, features, 0))
    scale = lax.rsqrt(squares / (features * 8) + 1e-06)
    gated = (jax.nn.silu(gate * scale) * (up * scale)).astype(jnp.bfloat16)

    def partial_for(x, core):
        columns = lax.dynamic_slice_in_dim(down_weight[0], (x * 2 + core) * features, features, 1)
        return dot(gated, columns)

    summed = summed_over_head(partial_for).astype(jnp.bfloat16)
    returned = lax.all_to_all(
        summed.reshape(experts_count, capacity, features), CTX, split_axis=0, concat_axis=0, tiled=True
    ).reshape(rows, features)

    raw_weights = route_weights.astype(jnp.float32)
    share = raw_weights / jnp.sum(raw_weights, axis=1, keepdims=True)
    spread = sum(
        jnp.where(place[:, k][:, None] == row_order[None, :], share[:, k][:, None], 0.0) for k in (0, 1)
    )
    coarse = lax.reduce_precision(spread, 8, 7)
    fine = (spread - coarse).astype(jnp.bfloat16)
    weighted = dot(coarse.astype(jnp.bfloat16), returned) + dot(fine, returned)
    return (hidden + weighted).astype(jnp.bfloat16)


def solution(mesh):
    torus = Mesh(mesh.devices.reshape(8, 4, 4, 2), (*CTX, *HEAD))
    in_specs = (
        P(CTX, HEAD),
        P(CTX, HEAD),
        P(CTX, HEAD),
        P(),
        P(HEAD),
        P(HEAD, CTX),
        P(CTX, HEAD),
        P(HEAD),
        P(CTX, None),
        P(CTX, None),
        P(CTX, None, HEAD),
        P(CTX, None, HEAD),
        P(CTX, HEAD, None),
    )
    return jax.shard_map(
        on_device, mesh=torus, in_specs=in_specs, out_specs=P(CTX, HEAD), check_vma=False
    )
```

```python
import functools

import jax
import jax.numpy as jnp
from jax import lax
from jax.experimental import pallas as pl
from jax.experimental.pallas import tpu as pltpu
from jax.sharding import Mesh
from jax.sharding import PartitionSpec as P

HEAD_DIM = 128
LONGEST = 4096
CTX = ("z", "y")
HEAD = ("x", "core")

highest = lax.Precision.HIGHEST


def shift(value, axis, step):
    size = lax.axis_size(axis)
    return lax.ppermute(value, axis, [(i, (i + step) % size) for i in range(size)])


def gathered_over_y(block):
    size, me = lax.axis_size("y"), lax.axis_index("y")
    return [(me, block)] + [((me - step) % size, shift(block, "y", step)) for step in (1, -1, 2)]


def gathered_over_z(block):
    size, me = lax.axis_size("z"), lax.axis_index("z")
    return [(me, block)] + [((me - step) % size, shift(block, "z", step)) for step in (1, -1, 2, -2, 3, -3, 4)]


def laid_out(pieces, size, dim=0):
    first = pieces[0][1]
    shape = first.shape[:dim] + (size,) + first.shape[dim:]
    buffer = jnp.zeros(shape, first.dtype)
    for index, piece in pieces:
        buffer = lax.dynamic_update_slice_in_dim(buffer, jnp.expand_dims(piece, dim), index, dim)
    return buffer


def episode_of(positions, lengths):
    count = lengths.shape[0]
    ahead = jnp.arange(count)[:, None] > jnp.arange(count)[None, :]
    starts = jnp.sum(jnp.where(ahead, lengths[None, :], 0), axis=1)
    return jnp.sum((starts[None, :] <= positions[:, None]).astype(jnp.int32), axis=1) - 1


def weight_and_prior_state(weight, state, last):
    step_together = lax.optimization_barrier
    depth = weight.shape[1] // 2
    size, me = lax.axis_size("z"), lax.axis_index("z")
    goal = last(1)
    first = gathered_over_y(weight[:, :depth])
    second = gathered_over_z(weight[:, depth:])
    sent = state.astype(jnp.bfloat16)
    sent, first = step_together((sent, first))
    slab = laid_out(first, lax.axis_size("y")).reshape(-1, depth)

    total = 0.0
    for step in (1, 2, 3, 4):
        total = total + jnp.where(last(step) == goal, shift(sent, CTX, step).astype(jnp.float32), 0.0)
    found = [(me, slab)]
    up, down = shift(slab, "z", 1), shift(slab, "z", -1)
    near, up, down, second = step_together((total.astype(jnp.bfloat16), up, down, second))
    found += [((me - 1) % size, up), ((me + 1) % size, down)]

    second = gathered_over_y(laid_out(second, size))
    up, down = shift(up, "z", 1), shift(down, "z", -1)
    far = shift(near, CTX, 4).astype(jnp.float32)
    total = total + jnp.where(last(5) == goal, far, 0.0)
    near, up, down = step_together((total.astype(jnp.bfloat16), up, down))
    found += [((me - 2) % size, up), ((me + 2) % size, down)]

    up, down = shift(up, "z", 1), shift(down, "z", -1)
    far = shift(near, CTX, 8).astype(jnp.float32)
    total = total + jnp.where(last(9) == goal, far, 0.0)
    found += [((me - 3) % size, up), ((me + 3) % size, down)]

    half = slab.shape[0] // 2
    opposite = jnp.concatenate([shift(up[:half], "z", 1), shift(down[half:], "z", -1)])
    found += [((me + 4) % size, opposite)]
    return (laid_out(found, size), laid_out(second, lax.axis_size("y"), 1)), total


def halves(value):
    middle = value.shape[0] // 2
    return value[:middle], value[middle:]


def summed_over_head(part):
    x, core = lax.axis_index("x"), lax.axis_index("core")
    narrow = lambda value: value.astype(jnp.bfloat16)
    wide = lambda value: value.astype(jnp.float32)

    def pair(distance):
        target = (x + distance) % 4
        other = shift(narrow(part(target, 1 - core)), "core", 1)
        return halves(wide(part(target, core)) + wide(other))

    top, low = pair(2)
    above, below = shift(narrow(top), "x", 1), shift(narrow(low), "x", -1)
    up_top, up_low = pair(1)
    up_low = shift(narrow(up_low), "x", 1)
    down_top, down_low = pair(3)
    down_top = shift(narrow(down_top), "x", -1)
    up_top = shift(narrow(up_top + wide(above)), "x", 1)
    down_low = shift(narrow(down_low + wide(below)), "x", -1)
    top, low = pair(0)
    return top + wide(up_top) + wide(down_top), low + wide(up_low) + wide(down_low)


def in_order_over_head(value):
    pair = jnp.stack([value, shift(value, "core", 1)])
    return [part for near in (pair, shift(pair, "x", 1), shift(pair, "x", -1), shift(pair, "x", 2)) for part in near]


def blocks_over_head(block):
    x, core = lax.axis_index("x"), lax.axis_index("core")
    top, low = halves(block)
    up_top, down_low = shift(top, "x", 1), shift(low, "x", -1)
    up_low, down_top = shift(low, "x", 1), shift(top, "x", -1)
    far_top, far_low = shift(up_top, "x", 1), shift(down_low, "x", -1)
    found = []
    for source, parts in (
        (x, (top, low)),
        ((x + 3) % 4, (up_top, up_low)),
        ((x + 1) % 4, (down_top, down_low)),
        ((x + 2) % 4, (far_top, far_low)),
    ):
        found.append((source * 2 + core, parts))
        found.append((source * 2 + 1 - core, tuple(shift(part, "core", 1) for part in parts)))
    return found


def products_kernel(count, last, sources, *refs):
    blocks, (inverses, *refs) = refs[: 2 * count], refs[2 * count :]
    gates, ups, refs = refs[:count], refs[count : 2 * count], refs[2 * count :]
    if last:
        gate_in, up_in, squares_in, gated, scale = refs
    else:
        gate_out, up_out, squares_out = refs
    rows = blocks[0].shape[0]
    weight = jnp.concatenate(
        [jnp.concatenate([g[...] for g in gates], 0), jnp.concatenate([u[...] for u in ups], 0)], 1
    )
    tile = weight.shape[1] // 2
    for part in range(2):
        at = pl.ds(part * rows, rows)

        @pl.when(pl.program_id(0) == 0)
        def _():
            squares = 0.0
            for i in range(count):
                wide = blocks[2 * i + part][...].astype(jnp.float32)
                squares = squares + wide * wide * inverses[i]
            squares = jnp.sum(squares, axis=1, keepdims=True)
            if last:
                squares = squares + squares_in[at, :]
                scale[at, :] = lax.rsqrt(squares / (8 * blocks[0].shape[1]) + 1e-06)
            else:
                squares_out[at, :] = squares

        taken = jnp.concatenate([blocks[2 * i + part][...] for i in range(count)], 1)
        both = jnp.dot(taken, weight, preferred_element_type=jnp.float32)
        gate, up = both[:, :tile], both[:, tile:]
        if last:
            gate = (gate + gate_in[at, :]) * scale[at, :]
            up = (up + up_in[at, :]) * scale[at, :]
            gated[at, :] = (gate / (1.0 + jnp.exp(-gate)) * up).astype(jnp.bfloat16)
        else:
            gate_out[at, :] = gate
            up_out[at, :] = up


def products(found, inverses, gate_weight, up_weight, before=None):
    count = len(found)
    features = inverses.shape[2]
    hidden = gate_weight.shape[1]
    rows = 2 * found[0][1][0].shape[0]
    tile = min(128, hidden)
    sources = jnp.stack([source for source, _ in found]).astype(jnp.int32)
    blocks = [half for _, parts in found for half in parts]
    whole = lambda shape: pl.BlockSpec(shape, lambda n, s: (0,) * len(shape))
    column = pl.BlockSpec((rows, tile), lambda n, s: (0, n))
    weights = [pl.BlockSpec((features, tile), lambda n, s, i=i: (s[i], n)) for i in range(count)]
    in_specs = [whole(half.shape) for half in blocks] + [whole(inverses.shape)] + weights + weights
    operands = [*blocks, inverses, *[gate_weight] * count, *[up_weight] * count]
    if before is None:
        out_shape = [jax.ShapeDtypeStruct((rows, hidden), jnp.float32)] * 2 + [
            jax.ShapeDtypeStruct((rows, 1), jnp.float32)
        ]
        out_specs = [column, column, whole((rows, 1))]
        scratch = []
    else:
        in_specs += [column, column, whole((rows, 1))]
        operands += before
        out_shape = jax.ShapeDtypeStruct((rows, hidden), jnp.bfloat16)
        out_specs = column
        scratch = [pltpu.VMEM((rows, 1), jnp.float32)]
    return pl.pallas_call(
        functools.partial(products_kernel, count, before is not None),
        out_shape=out_shape,
        grid_spec=pltpu.PrefetchScalarGridSpec(
            num_scalar_prefetch=1,
            grid=(hidden // tile,),
            in_specs=in_specs,
            out_specs=out_specs,
            scratch_shapes=scratch,
        ),
        compiler_params=pltpu.CompilerParams(vmem_limit_bytes=40 * 1024 * 1024),
        cost_estimate=pl.CostEstimate(
            flops=4 * rows * count * features * hidden,
            bytes_accessed=4 * count * features * hidden + 8 * rows * hidden,
            transcendentals=0,
        ),
    )(sources, *operands)


def dot(a, b):
    return jnp.dot(a, b, preferred_element_type=jnp.float32)


def on_device(
    query,
    key,
    value,
    episode_lengths,
    attn_gain,
    out_weight,
    residual,
    norm_gain,
    expert_ids,
    route_weights,
    gate_weight,
    up_weight,
    down_weight,
):
    tok_rows = query.shape[0]
    heads_local = query.shape[1] // HEAD_DIM
    features = residual.shape[1]
    own_index = lax.axis_index(CTX)
    experts_count = gate_weight.shape[0] * lax.axis_size(CTX)
    capacity = 3 * tok_rows // experts_count
    rows = experts_count * capacity

    positions = own_index * tok_rows + jnp.arange(tok_rows, dtype=jnp.int32)
    episode = episode_of(positions, episode_lengths)
    lasts = episode_of((own_index + 1 - jnp.arange(LONGEST // tok_rows + 2, dtype=jnp.int32)) * tok_rows - 1, episode_lengths)
    final, prior = lasts[0], lasts[1]
    lifted_query = jax.nn.silu(query.astype(jnp.float32)).reshape(tok_rows, heads_local, HEAD_DIM)
    lifted_key = jax.nn.silu(key.astype(jnp.float32)).reshape(tok_rows, heads_local, HEAD_DIM)
    value_rows = value.astype(jnp.float32).reshape(tok_rows, heads_local, HEAD_DIM)
    keep = (episode == final).astype(jnp.float32)
    state = jnp.einsum("shd,she->hde", lifted_key * keep[:, None, None], value_rows, precision=highest)
    (first_rows, second_rows), carry_state = weight_and_prior_state(out_weight.T, state, lambda back: lasts[back])
    order = jnp.arange(tok_rows, dtype=jnp.int32)
    allowed = ((order[:, None] >= order[None, :]) & (episode[:, None] == episode[None, :])).astype(
        jnp.float32
    )
    scores = jnp.einsum("thd,shd->hts", lifted_query, lifted_key, precision=highest)
    inside = jnp.einsum("hts,shd->thd", scores * allowed[None], value_rows, precision=highest)
    outside = jnp.einsum("thd,hde->the", lifted_query, carry_state, precision=highest)
    attn = inside + outside * (episode == prior).astype(jnp.float32)[:, None, None]
    mean_square = jnp.mean(attn * attn, axis=2, keepdims=True)
    scaled = attn * lax.rsqrt(mean_square + 1e-06) * attn_gain.reshape(heads_local, HEAD_DIM)
    headed = scaled.reshape(tok_rows, heads_local * HEAD_DIM).astype(jnp.bfloat16)

    depth = first_rows.shape[2]
    across = (((1,), (1,)), ((), ()))

    def mixed_for(x, core):
        first = lax.dynamic_index_in_dim(first_rows, x * 2 + core, 0, keepdims=False)
        second = lax.dynamic_index_in_dim(second_rows, x * 2 + core, 0, keepdims=False).reshape(first.shape)
        return lax.dot_general(
            headed[:, :depth], first, across, preferred_element_type=jnp.float32
        ) + lax.dot_general(headed[:, depth:], second, across, preferred_element_type=jnp.float32)

    hidden = residual.astype(jnp.float32) + jnp.concatenate(summed_over_head(mixed_for))
    scaled_rows = (hidden * norm_gain).astype(jnp.bfloat16)

    flat_ids = expert_ids.reshape(-1)
    pair_order = jnp.arange(flat_ids.shape[0])
    same = (flat_ids[:, None] == flat_ids[None, :]) & (pair_order[:, None] > pair_order[None, :])
    slot = jnp.sum(same.astype(jnp.int32), axis=1)
    place = (flat_ids * capacity + slot).reshape(tok_rows, 2)
    row_order = jnp.arange(rows, dtype=jnp.int32)
    chosen = (row_order[:, None] == place[:, 0][None, :]) | (row_order[:, None] == place[:, 1][None, :])
    outgoing = dot(chosen.astype(jnp.bfloat16), scaled_rows).astype(jnp.bfloat16)
    arrived = lax.all_to_all(
        outgoing.reshape(experts_count, capacity, features), CTX, split_axis=0, concat_axis=0, tiled=True
    ).reshape(rows, features)

    inverses = jnp.stack(in_order_over_head(1.0 / (norm_gain * norm_gain))).reshape(8, 1, features)
    found = blocks_over_head(arrived)
    before = products(found[:6], inverses[:6], gate_weight[0], up_weight[0])
    gated = products(found[6:], inverses[6:], gate_weight[0], up_weight[0], before)

    def partial_for(x, core):
        columns = lax.dynamic_slice_in_dim(down_weight[0], (x * 2 + core) * features, features, 1)
        return dot(gated, columns)

    summed = jnp.concatenate(summed_over_head(partial_for)).astype(jnp.bfloat16)
    returned = lax.all_to_all(
        summed.reshape(experts_count, capacity, features), CTX, split_axis=0, concat_axis=0, tiled=True
    ).reshape(rows, features)

    raw_weights = route_weights.astype(jnp.float32)
    share = raw_weights / jnp.sum(raw_weights, axis=1, keepdims=True)
    spread = sum(
        jnp.where(place[:, k][:, None] == row_order[None, :], share[:, k][:, None], 0.0) for k in (0, 1)
    )
    coarse = lax.reduce_precision(spread, 8, 7)
    fine = (spread - coarse).astype(jnp.bfloat16)
    weighted = dot(coarse.astype(jnp.bfloat16), returned) + dot(fine, returned)
    return (hidden + weighted).astype(jnp.bfloat16)


def solution(mesh):
    torus = Mesh(mesh.devices.reshape(8, 4, 4, 2), (*CTX, *HEAD))
    in_specs = (
        P(CTX, HEAD),
        P(CTX, HEAD),
        P(CTX, HEAD),
        P(),
        P(HEAD),
        P(HEAD, CTX),
        P(CTX, HEAD),
        P(HEAD),
        P(CTX, None),
        P(CTX, None),
        P(CTX, None, HEAD),
        P(CTX, None, HEAD),
        P(CTX, HEAD, None),
    )
    return jax.shard_map(
        on_device, mesh=torus, in_specs=in_specs, out_specs=P(CTX, HEAD), check_vma=False
    )
```

```python
import jax
import jax.numpy as jnp
from jax import lax
from jax.sharding import Mesh
from jax.sharding import PartitionSpec as P

HEAD_DIM = 128
LONGEST = 4096
CTX = ("z", "y")
HEAD = ("x", "core")

highest = lax.Precision.HIGHEST


def shift(value, axis, step):
    size = lax.axis_size(axis)
    return lax.ppermute(value, axis, [(i, (i + step) % size) for i in range(size)])


def gathered_over_y(block):
    size, me = lax.axis_size("y"), lax.axis_index("y")
    return [(me, block)] + [((me - step) % size, shift(block, "y", step)) for step in (1, -1, 2)]


def laid_out(pieces, size):
    first = pieces[0][1]
    buffer = jnp.zeros((size, *first.shape), first.dtype)
    for index, piece in pieces:
        buffer = lax.dynamic_update_slice_in_dim(buffer, piece[None], index, 0)
    return buffer


def episode_of(positions, lengths):
    count = lengths.shape[0]
    ahead = jnp.arange(count)[:, None] > jnp.arange(count)[None, :]
    starts = jnp.sum(jnp.where(ahead, lengths[None, :], 0), axis=1)
    return jnp.sum((starts[None, :] <= positions[:, None]).astype(jnp.int32), axis=1) - 1


def exchanged_ahead(weight, state, gain, last):
    step_together = lax.optimization_barrier
    size, me = lax.axis_size("z"), lax.axis_index("z")
    core = lax.axis_index("core")
    goal = last(1)
    narrow = lambda value: value.astype(jnp.bfloat16)
    joined = lambda total, far, back: total + jnp.where(last(back) == goal, far.astype(jnp.float32), 0.0)

    first = gathered_over_y(weight)
    sent, first = step_together((narrow(state), first))
    slab = laid_out(first, lax.axis_size("y")).reshape(-1, weight.shape[1])

    up, down = shift(slab, "z", 1), shift(slab, "z", -1)
    total = joined(joined(0.0, shift(sent, CTX, 1), 1), shift(sent, CTX, 2), 2)
    other = shift(gain, "core", 1)
    near, up, down, other = step_together((narrow(total), up, down, other))
    found = [(me, slab), ((me - 1) % size, up), ((me + 1) % size, down)]

    up, down = shift(up, "z", 1), shift(down, "z", -1)
    total = joined(total, shift(near, CTX, 2), 3)
    pair = jnp.where(core == 0, jnp.stack([gain, other]), jnp.stack([other, gain]))
    pairs = [pair, shift(pair, "x", 1), shift(pair, "x", -1), shift(pair, "x", 2)]
    near, up, down, pairs = step_together((narrow(total), up, down, pairs))
    found += [((me - 2) % size, up), ((me + 2) % size, down)]

    up, down = shift(up, "z", 1), shift(down, "z", -1)
    total = joined(total, shift(near, CTX, 4), 5)
    near, up, down = step_together((narrow(total), up, down))
    found += [((me - 3) % size, up), ((me + 3) % size, down)]

    half = slab.shape[0] // 2
    opposite = jnp.concatenate([shift(up[:half], "z", 1), shift(down[half:], "z", -1)])
    total = joined(total, shift(near, CTX, 8), 9)
    found += [((me + 4) % size, opposite)]
    x = lax.axis_index("x")
    gains = laid_out([((x - step) % 4, pair) for step, pair in zip((0, 1, -1, 2), pairs)], 4)
    return laid_out(found, size), total, gains.reshape(1, -1)


def halves(value):
    middle = value.shape[0] // 2
    return value[:middle], value[middle:]


def narrow(value):
    return value.astype(jnp.bfloat16)


def wide(value):
    return value.astype(jnp.float32)


def summed_over_head(source, part, in_halves):
    x, core = lax.axis_index("x"), lax.axis_index("core")

    def pair(distance):
        target = (x + distance) % 4
        other = shift(narrow(part(source, target, 1 - core)), "core", 1)
        return part(source, target, core) + wide(other)

    far = narrow(pair(2))
    if in_halves:
        far, source = lax.optimization_barrier((far, source))
    top, low = halves(far)
    above, below = shift(top, "x", 1), shift(low, "x", -1)
    up_top, up_low = halves(pair(1))
    down_top, down_low = halves(pair(3))
    if in_halves:
        up_low = shift(narrow(up_low), "x", 1)
        down_top = shift(narrow(down_top), "x", -1)
        up_top = shift(narrow(up_top + wide(above)), "x", 1)
        down_low = shift(narrow(down_low + wide(below)), "x", -1)
        top, low = halves(pair(0))
        return jnp.concatenate([top + wide(up_top) + wide(down_top), low + wide(up_low) + wide(down_low)])
    up = shift(jnp.concatenate([narrow(up_top + wide(above)), narrow(up_low)]), "x", 1)
    down = shift(jnp.concatenate([narrow(down_top), narrow(down_low + wide(below))]), "x", -1)
    return pair(0) + wide(up) + wide(down)


def whole_rows(block):
    x, core = lax.axis_index("x"), lax.axis_index("core")
    rows, features = block.shape
    half = rows // 2
    up, down = shift(block, "x", 1), shift(block, "x", -1)
    far = jnp.concatenate([shift(up[:half], "x", 1), shift(down[half:], "x", -1)])
    whole = jnp.zeros((rows, features * 8), block.dtype)
    for source, part in ((x, block), ((x + 3) % 4, up), ((x + 1) % 4, down), ((x + 2) % 4, far)):
        whole = lax.dynamic_update_slice_in_dim(whole, part, (source * 2 + core) * features, 1)
        other = shift(part, "core", 1)
        whole = lax.dynamic_update_slice_in_dim(whole, other, (source * 2 + 1 - core) * features, 1)
    return whole


def dot(a, b):
    return jnp.dot(a, b, preferred_element_type=jnp.float32)


def on_device(
    query,
    key,
    value,
    episode_lengths,
    attn_gain,
    out_weight,
    residual,
    norm_gain,
    expert_ids,
    route_weights,
    gate_weight,
    up_weight,
    down_weight,
):
    tok_rows = query.shape[0]
    heads_local = query.shape[1] // HEAD_DIM
    features = residual.shape[1]
    own_index = lax.axis_index(CTX)
    experts_count = gate_weight.shape[0] * lax.axis_size(CTX)
    capacity = 3 * tok_rows // experts_count
    rows = experts_count * capacity

    positions = own_index * tok_rows + jnp.arange(tok_rows, dtype=jnp.int32)
    episode = episode_of(positions, episode_lengths)
    lasts = episode_of((own_index + 1 - jnp.arange(LONGEST // tok_rows + 2, dtype=jnp.int32)) * tok_rows - 1, episode_lengths)
    final, prior = lasts[0], lasts[1]
    lifted_query = jax.nn.silu(query.astype(jnp.float32)).reshape(tok_rows, heads_local, HEAD_DIM)
    lifted_key = jax.nn.silu(key.astype(jnp.float32)).reshape(tok_rows, heads_local, HEAD_DIM)
    value_rows = value.astype(jnp.float32).reshape(tok_rows, heads_local, HEAD_DIM)
    keep = (episode == final).astype(jnp.float32)
    state = jnp.einsum("shd,she->hde", lifted_key * keep[:, None, None], value_rows, precision=highest)
    whole_weight, carry_state, gains = exchanged_ahead(out_weight.T, state, norm_gain, lambda back: lasts[back])
    order = jnp.arange(tok_rows, dtype=jnp.int32)
    allowed = ((order[:, None] >= order[None, :]) & (episode[:, None] == episode[None, :])).astype(
        jnp.float32
    )
    scores = jnp.einsum("thd,shd->hts", lifted_query, lifted_key, precision=highest)
    inside = jnp.einsum("hts,shd->thd", scores * allowed[None], value_rows, precision=highest)
    outside = jnp.einsum("thd,hde->the", lifted_query, carry_state, precision=highest)
    attn = inside + outside * (episode == prior).astype(jnp.float32)[:, None, None]
    mean_square = jnp.mean(attn * attn, axis=2, keepdims=True)
    scaled = attn * lax.rsqrt(mean_square + 1e-06) * attn_gain.reshape(heads_local, HEAD_DIM)
    headed = scaled.reshape(tok_rows, heads_local * HEAD_DIM).astype(jnp.bfloat16)

    def mixed_for(headed, x, core):
        columns = lax.dynamic_index_in_dim(whole_weight, x * 2 + core, 0, keepdims=False)
        return lax.dot_general(headed, columns, (((1,), (1,)), ((), ())), preferred_element_type=jnp.float32)

    hidden = wide(residual) + summed_over_head(headed, mixed_for, False)
    scaled_rows = (hidden * norm_gain).astype(jnp.bfloat16)

    flat_ids = expert_ids.reshape(-1)
    pair_order = jnp.arange(flat_ids.shape[0])
    same = (flat_ids[:, None] == flat_ids[None, :]) & (pair_order[:, None] > pair_order[None, :])
    slot = jnp.sum(same.astype(jnp.int32), axis=1)
    place = (flat_ids * capacity + slot).reshape(tok_rows, 2)
    row_order = jnp.arange(rows, dtype=jnp.int32)
    chosen = (row_order[:, None] == place[:, 0][None, :]) | (row_order[:, None] == place[:, 1][None, :])
    outgoing = dot(chosen.astype(jnp.bfloat16), scaled_rows).astype(jnp.bfloat16)
    arrived = lax.all_to_all(
        outgoing.reshape(experts_count, capacity, features), CTX, split_axis=0, concat_axis=0, tiled=True
    ).reshape(rows, features)

    flat = whole_rows(arrived)
    squares = jnp.sum(jnp.square(wide(flat) / gains), axis=1, keepdims=True)
    scale = lax.rsqrt(squares / flat.shape[1] + 1e-06)
    gate, up = dot(flat, gate_weight[0]) * scale, dot(flat, up_weight[0]) * scale
    gated = narrow(jax.nn.silu(gate) * up)

    def partial_for(gated, x, core):
        columns = lax.dynamic_slice_in_dim(down_weight[0], (x * 2 + core) * features, features, 1)
        return dot(gated, columns)

    summed = narrow(summed_over_head(gated, partial_for, True))
    returned = lax.all_to_all(
        summed.reshape(experts_count, capacity, features), CTX, split_axis=0, concat_axis=0, tiled=True
    ).reshape(rows, features)

    raw_weights = route_weights.astype(jnp.float32)
    share = raw_weights / jnp.sum(raw_weights, axis=1, keepdims=True)
    spread = sum(
        jnp.where(place[:, k][:, None] == row_order[None, :], share[:, k][:, None], 0.0) for k in (0, 1)
    )
    coarse = lax.reduce_precision(spread, 8, 7)
    fine = (spread - coarse).astype(jnp.bfloat16)
    weighted = dot(coarse.astype(jnp.bfloat16), returned) + dot(fine, returned)
    return (hidden + weighted).astype(jnp.bfloat16)


def solution(mesh):
    torus = Mesh(mesh.devices.reshape(8, 4, 4, 2), (*CTX, *HEAD))
    in_specs = (
        P(CTX, HEAD),
        P(CTX, HEAD),
        P(CTX, HEAD),
        P(),
        P(HEAD),
        P(HEAD, CTX),
        P(CTX, HEAD),
        P(HEAD),
        P(CTX, None),
        P(CTX, None),
        P(CTX, None, HEAD),
        P(CTX, None, HEAD),
        P(CTX, HEAD, None),
    )
    return jax.shard_map(
        on_device, mesh=torus, in_specs=in_specs, out_specs=P(CTX, HEAD), check_vma=False
    )
```

```python
import jax
import jax.numpy as jnp
from jax import lax
from jax.sharding import Mesh
from jax.sharding import PartitionSpec as P

HEAD_DIM = 128
LONGEST = 4096
MET = (-1, 0, 1, 2)
CTX = ("z", "y")
HEAD = ("x", "core")

highest = lax.Precision.HIGHEST


def shift(value, axis, step):
    size = lax.axis_size(axis)
    return lax.ppermute(value, axis, [(i, (i + step) % size) for i in range(size)])


def gathered_over_y(block):
    size, me = lax.axis_size("y"), lax.axis_index("y")
    return [(me, block)] + [((me - step) % size, shift(block, "y", step)) for step in (1, -1, 2)]


def laid_out(pieces, size):
    first = pieces[0][1]
    buffer = jnp.zeros((size, *first.shape), first.dtype)
    for index, piece in pieces:
        buffer = lax.dynamic_update_slice_in_dim(buffer, piece[None], index, 0)
    return buffer


def episode_of(positions, lengths):
    count = lengths.shape[0]
    ahead = jnp.arange(count)[:, None] > jnp.arange(count)[None, :]
    starts = jnp.sum(jnp.where(ahead, lengths[None, :], 0), axis=1)
    return jnp.sum((starts[None, :] <= positions[:, None]).astype(jnp.int32), axis=1) - 1


def weight_and_prior_state(weight, state, last):
    size, me = lax.axis_size("z"), lax.axis_index("z")
    goal = last(1)
    joined = lambda total, far, back: total + jnp.where(last(back) == goal, wide(far), 0.0)

    def after(value, *others):
        return lax.optimization_barrier((value, *others))[0]

    first = gathered_over_y(weight)
    sent = after(narrow(state), *(part for _, part in first))
    slab = laid_out(first, lax.axis_size("y")).reshape(-1, weight.shape[1])

    up, down = shift(slab, "z", 1), shift(slab, "z", -1)
    total = joined(joined(0.0, shift(sent, CTX, 1), 1), shift(sent, CTX, 2), 2)
    near = after(narrow(total), up, down)
    found = [(me, slab), ((me - 1) % size, up), ((me + 1) % size, down)]

    up, down = shift(up, "z", 1), shift(down, "z", -1)
    total = joined(total, shift(near, CTX, 2), 3)
    near = after(narrow(total), up, down)
    found += [((me - 2) % size, up), ((me + 2) % size, down)]

    up, down = shift(up, "z", 1), shift(down, "z", -1)
    total = joined(total, shift(near, CTX, 4), 5)
    near = after(narrow(total), up, down)
    found += [((me - 3) % size, up), ((me + 3) % size, down)]

    half = slab.shape[0] // 2
    opposite = jnp.concatenate([shift(up[:half], "z", 1), shift(down[half:], "z", -1)])
    total = joined(total, shift(near, CTX, 8), 9)
    found += [((me + 4) % size, opposite)]
    return laid_out(found, size), total


def halves(value):
    middle = value.shape[0] // 2
    return value[:middle], value[middle:]


def narrow(value):
    return value.astype(jnp.bfloat16)


def wide(value):
    return value.astype(jnp.float32)


def summed_over_head(source, part, in_halves):
    def pair(distance):
        return part(source, distance, True) + wide(shift(narrow(part(source, distance, False)), "core", 1))

    first = narrow(part(source, 2, False))
    first, source = lax.optimization_barrier((first, source))
    top, low = halves(narrow(part(source, 2, True) + wide(shift(first, "core", 1))))
    above, below = shift(top, "x", 1), shift(low, "x", -1)
    up_top, up_low = halves(pair(1))
    down_top, down_low = halves(pair(3))
    if in_halves:
        up_low = shift(narrow(up_low), "x", 1)
        down_top = shift(narrow(down_top), "x", -1)
        up_top = shift(narrow(up_top + wide(above)), "x", 1)
        down_low = shift(narrow(down_low + wide(below)), "x", -1)
        top, low = halves(pair(0))
        return jnp.concatenate([top + wide(up_top) + wide(down_top), low + wide(up_low) + wide(down_low)])
    up = shift(jnp.concatenate([narrow(up_top + wide(above)), narrow(up_low)]), "x", 1)
    down = shift(jnp.concatenate([narrow(down_top), narrow(down_low + wide(below))]), "x", -1)
    return pair(0) + wide(up) + wide(down)


def met(x, core):
    return [((x + distance) % 4) * 2 + place for distance in MET for place in (core, 1 - core)]


def gathered_gains(gain):
    pair = jnp.stack([gain, shift(gain, "core", 1)])
    return jnp.concatenate([pair if d == 0 else shift(pair, "x", -d) for d in MET]).reshape(1, -1)


def rows_over_head(block):
    half = block.shape[0] // 2
    from_low, from_high = shift(block, "x", 1), shift(block, "x", -1)
    far = (shift(from_low[:half], "x", 1), shift(from_high[half:], "x", -1))
    with_other = lambda part: [part, shift(part, "core", 1)]
    return jnp.concatenate(with_other(from_low) + with_other(block) + with_other(from_high), 1), far


def dot(a, b):
    return jnp.dot(a, b, preferred_element_type=jnp.float32)


def on_device(
    query,
    key,
    value,
    episode_lengths,
    attn_gain,
    out_weight,
    residual,
    norm_gain,
    expert_ids,
    route_weights,
    gate_weight,
    up_weight,
    down_weight,
):
    tok_rows = query.shape[0]
    heads_local = query.shape[1] // HEAD_DIM
    features = residual.shape[1]
    own_index = lax.axis_index(CTX)
    experts_count = gate_weight.shape[0] * lax.axis_size(CTX)
    capacity = 3 * tok_rows // experts_count
    rows = experts_count * capacity

    positions = own_index * tok_rows + jnp.arange(tok_rows, dtype=jnp.int32)
    episode = episode_of(positions, episode_lengths)
    lasts = episode_of((own_index + 1 - jnp.arange(LONGEST // tok_rows + 2, dtype=jnp.int32)) * tok_rows - 1, episode_lengths)
    final, prior = lasts[0], lasts[1]
    lifted_query = jax.nn.silu(query.astype(jnp.float32)).reshape(tok_rows, heads_local, HEAD_DIM)
    lifted_key = jax.nn.silu(key.astype(jnp.float32)).reshape(tok_rows, heads_local, HEAD_DIM)
    value_rows = value.astype(jnp.float32).reshape(tok_rows, heads_local, HEAD_DIM)
    keep = (episode == final).astype(jnp.float32)
    state = jnp.einsum("shd,she->hde", lifted_key * keep[:, None, None], value_rows, precision=highest)
    whole_weight, carry_state = weight_and_prior_state(out_weight.T, state, lambda back: lasts[back])
    order = jnp.arange(tok_rows, dtype=jnp.int32)
    allowed = ((order[:, None] >= order[None, :]) & (episode[:, None] == episode[None, :])).astype(
        jnp.float32
    )
    scores = jnp.einsum("thd,shd->hts", lifted_query, lifted_key, precision=highest)
    inside = jnp.einsum("hts,shd->thd", scores * allowed[None], value_rows, precision=highest)
    outside = jnp.einsum("thd,hde->the", lifted_query, carry_state, precision=highest)
    attn = inside + outside * (episode == prior).astype(jnp.float32)[:, None, None]
    mean_square = jnp.mean(attn * attn, axis=2, keepdims=True)
    scaled = attn * lax.rsqrt(mean_square + 1e-06) * attn_gain.reshape(heads_local, HEAD_DIM)
    headed = scaled.reshape(tok_rows, heads_local * HEAD_DIM).astype(jnp.bfloat16)

    x, core = lax.axis_index("x"), lax.axis_index("core")

    def mixed_for(headed, distance, same):
        target = ((x + distance) % 4) * 2 + (core if same else 1 - core)
        columns = lax.dynamic_index_in_dim(whole_weight, target, 0, keepdims=False)
        return lax.dot_general(headed, columns, (((1,), (1,)), ((), ())), preferred_element_type=jnp.float32)

    hidden = wide(residual) + summed_over_head(headed, mixed_for, False)
    scaled_rows = (hidden * norm_gain).astype(jnp.bfloat16)

    flat_ids = expert_ids.reshape(-1)
    pair_order = jnp.arange(flat_ids.shape[0])
    same = (flat_ids[:, None] == flat_ids[None, :]) & (pair_order[:, None] > pair_order[None, :])
    slot = jnp.sum(same.astype(jnp.int32), axis=1)
    place = (flat_ids * capacity + slot).reshape(tok_rows, 2)
    row_order = jnp.arange(rows, dtype=jnp.int32)
    chosen = (row_order[:, None] == place[:, 0][None, :]) | (row_order[:, None] == place[:, 1][None, :])
    outgoing = dot(chosen.astype(jnp.bfloat16), scaled_rows).astype(jnp.bfloat16)
    outgoing, late_x, late_gain = lax.optimization_barrier((outgoing, x, norm_gain))
    arrived = lax.all_to_all(
        outgoing.reshape(experts_count, capacity, features), CTX, split_axis=0, concat_axis=0, tiled=True
    ).reshape(rows, features)
    order_met = met(late_x, core)
    pieces = lambda weight, dim: [
        lax.dynamic_slice_in_dim(weight, source * features, features, dim) for source in order_met
    ]
    gains = gathered_gains(late_gain)
    gate_rows = jnp.concatenate(pieces(gate_weight[0], 0))
    up_rows = jnp.concatenate(pieces(up_weight[0], 0))
    down_columns = jnp.stack(pieces(down_weight[0], 1))
    arrived, gains, gate_rows, up_rows, down_columns = lax.optimization_barrier(
        (arrived, gains, gate_rows, up_rows, down_columns)
    )

    near, far = rows_over_head(arrived)
    depth = near.shape[1]
    squared = lambda part, gain: jnp.sum(jnp.square(wide(part) / gain), axis=1, keepdims=True)
    gate_near, up_near, squares, far = lax.optimization_barrier(
        (dot(near, gate_rows[:depth]), dot(near, up_rows[:depth]), squared(near, gains[:, :depth]), far)
    )
    far = jnp.concatenate(far)
    far = jnp.concatenate([far, shift(far, "core", 1)], 1)
    squares = squares + squared(far, gains[:, depth:])
    scale = lax.rsqrt(squares / gains.shape[1] + 1e-06)
    gate = (gate_near + dot(far, gate_rows[depth:])) * scale
    up = (up_near + dot(far, up_rows[depth:])) * scale
    gated = narrow(jax.nn.silu(gate) * up)

    def partial_for(gated, distance, same):
        at = [d % 4 for d in MET].index(distance) * 2 + (0 if same else 1)
        return dot(gated, down_columns[at])

    summed = narrow(summed_over_head(gated, partial_for, True))
    returned = lax.all_to_all(
        summed.reshape(experts_count, capacity, features), CTX, split_axis=0, concat_axis=0, tiled=True
    ).reshape(rows, features)

    raw_weights = route_weights.astype(jnp.float32)
    share = raw_weights / jnp.sum(raw_weights, axis=1, keepdims=True)
    spread = sum(
        jnp.where(place[:, k][:, None] == row_order[None, :], share[:, k][:, None], 0.0) for k in (0, 1)
    )
    coarse = lax.reduce_precision(spread, 8, 7)
    fine = (spread - coarse).astype(jnp.bfloat16)
    weighted = dot(coarse.astype(jnp.bfloat16), returned) + dot(fine, returned)
    return (hidden + weighted).astype(jnp.bfloat16)


def solution(mesh):
    torus = Mesh(mesh.devices.reshape(8, 4, 4, 2), (*CTX, *HEAD))
    in_specs = (
        P(CTX, HEAD),
        P(CTX, HEAD),
        P(CTX, HEAD),
        P(),
        P(HEAD),
        P(HEAD, CTX),
        P(CTX, HEAD),
        P(HEAD),
        P(CTX, None),
        P(CTX, None),
        P(CTX, None, HEAD),
        P(CTX, None, HEAD),
        P(CTX, HEAD, None),
    )
    return jax.shard_map(
        on_device, mesh=torus, in_specs=in_specs, out_specs=P(CTX, HEAD), check_vma=False
    )
```

```python
import jax
import jax.numpy as jnp
from jax import lax
from jax.sharding import Mesh
from jax.sharding import PartitionSpec as P

HEAD_DIM = 128
LONGEST = 4096
CTX = ("z", "y")
HEAD = ("x", "core")

highest = lax.Precision.HIGHEST


def shift(value, axis, step):
    size = lax.axis_size(axis)
    return lax.ppermute(value, axis, [(i, (i + step) % size) for i in range(size)])


def gathered_over_y(block):
    size, me = lax.axis_size("y"), lax.axis_index("y")
    return [(me, block)] + [((me - step) % size, shift(block, "y", step)) for step in (1, -1, 2)]


def laid_out(pieces, size):
    first = pieces[0][1]
    buffer = jnp.zeros((size, *first.shape), first.dtype)
    for index, piece in pieces:
        buffer = lax.dynamic_update_slice_in_dim(buffer, piece[None], index, 0)
    return buffer


def episode_of(positions, lengths):
    count = lengths.shape[0]
    ahead = jnp.arange(count)[:, None] > jnp.arange(count)[None, :]
    starts = jnp.sum(jnp.where(ahead, lengths[None, :], 0), axis=1)
    return jnp.sum((starts[None, :] <= positions[:, None]).astype(jnp.int32), axis=1) - 1


def weight_and_prior_state(weight, state, last):
    size, me = lax.axis_size("z"), lax.axis_index("z")
    goal = last(1)
    joined = lambda total, far, back: total + jnp.where(last(back) == goal, wide(far), 0.0)

    def after(value, *others):
        return lax.optimization_barrier((value, *others))[0]

    first = gathered_over_y(weight)
    sent = after(narrow(state), *(part for _, part in first))
    slab = laid_out(first, lax.axis_size("y")).reshape(-1, weight.shape[1])

    up, down = shift(slab, "z", 1), shift(slab, "z", -1)
    total = joined(joined(0.0, shift(sent, CTX, 1), 1), shift(sent, CTX, 2), 2)
    near = after(narrow(total), up, down)
    found = [(me, slab), ((me - 1) % size, up), ((me + 1) % size, down)]

    up, down = shift(up, "z", 1), shift(down, "z", -1)
    total = joined(total, shift(near, CTX, 2), 3)
    near = after(narrow(total), up, down)
    found += [((me - 2) % size, up), ((me + 2) % size, down)]

    up, down = shift(up, "z", 1), shift(down, "z", -1)
    total = joined(total, shift(near, CTX, 4), 5)
    near = after(narrow(total), up, down)
    found += [((me - 3) % size, up), ((me + 3) % size, down)]

    half = slab.shape[0] // 2
    opposite = jnp.concatenate([shift(up[:half], "z", 1), shift(down[half:], "z", -1)])
    total = joined(total, shift(near, CTX, 8), 9)
    found += [((me + 4) % size, opposite)]
    return laid_out(found, size), total


def halves(value):
    middle = value.shape[0] // 2
    return value[:middle], value[middle:]


def narrow(value):
    return value.astype(jnp.bfloat16)


def wide(value):
    return value.astype(jnp.float32)


def summed_over_head(source, part, in_halves):
    def pair(distance):
        return wide(part(source, distance, True)) + wide(shift(narrow(part(source, distance, False)), "core", 1))

    first = narrow(part(source, 2, False))
    first, source = lax.optimization_barrier((first, source))
    far = narrow(wide(part(source, 2, True)) + wide(shift(first, "core", 1)))
    if in_halves:
        far, source = lax.optimization_barrier((far, source))
    top, low = halves(far)
    above, below = shift(top, "x", 1), shift(low, "x", -1)
    up_top, up_low = halves(pair(1))
    down_top, down_low = halves(pair(3))
    if in_halves:
        up_low = shift(narrow(up_low), "x", 1)
        down_top = shift(narrow(down_top), "x", -1)
        up_top = shift(narrow(up_top + wide(above)), "x", 1)
        down_low = shift(narrow(down_low + wide(below)), "x", -1)
        top, low = halves(pair(0))
        return jnp.concatenate([top + wide(up_top) + wide(down_top), low + wide(up_low) + wide(down_low)])
    up = shift(jnp.concatenate([narrow(up_top + wide(above)), narrow(up_low)]), "x", 1)
    down = shift(jnp.concatenate([narrow(down_top), narrow(down_low + wide(below))]), "x", -1)
    return pair(0) + wide(up) + wide(down)


def gathered_gains(gain):
    x, core = lax.axis_index("x"), lax.axis_index("core")
    other = shift(gain, "core", 1)
    pair = jnp.where(core == 0, jnp.stack([gain, other]), jnp.stack([other, gain]))
    found = [((x - step) % 4, shift(pair, "x", step) if step else pair) for step in (0, 1, -1, 2)]
    return laid_out(found, 4).reshape(1, -1)


def rows_over_head(block):
    x, core = lax.axis_index("x"), lax.axis_index("core")
    rows, features = block.shape
    half = rows // 2
    from_low, from_high = shift(block, "x", 1), shift(block, "x", -1)
    far = (shift(from_low[:half], "x", 1), shift(from_high[half:], "x", -1))
    near = jnp.zeros((rows, features * 8), block.dtype)
    for source, part in ((x, block), ((x + 3) % 4, from_low), ((x + 1) % 4, from_high)):
        for place, piece in ((core, part), (1 - core, shift(part, "core", 1))):
            near = lax.dynamic_update_slice_in_dim(near, piece, (source * 2 + place) * features, 1)
    return near, far


def dot(a, b):
    return jnp.dot(a, b, preferred_element_type=jnp.float32)


def on_device(
    query,
    key,
    value,
    episode_lengths,
    attn_gain,
    out_weight,
    residual,
    norm_gain,
    expert_ids,
    route_weights,
    gate_weight,
    up_weight,
    down_weight,
):
    tok_rows = query.shape[0]
    heads_local = query.shape[1] // HEAD_DIM
    features = residual.shape[1]
    own_index = lax.axis_index(CTX)
    experts_count = gate_weight.shape[0] * lax.axis_size(CTX)
    capacity = 3 * tok_rows // experts_count
    rows = experts_count * capacity

    positions = own_index * tok_rows + jnp.arange(tok_rows, dtype=jnp.int32)
    episode = episode_of(positions, episode_lengths)
    lasts = episode_of((own_index + 1 - jnp.arange(LONGEST // tok_rows + 2, dtype=jnp.int32)) * tok_rows - 1, episode_lengths)
    final, prior = lasts[0], lasts[1]
    lifted_query = jax.nn.silu(query.astype(jnp.float32)).reshape(tok_rows, heads_local, HEAD_DIM)
    lifted_key = jax.nn.silu(key.astype(jnp.float32)).reshape(tok_rows, heads_local, HEAD_DIM)
    value_rows = value.astype(jnp.float32).reshape(tok_rows, heads_local, HEAD_DIM)
    keep = (episode == final).astype(jnp.float32)
    state = jnp.einsum("shd,she->hde", lifted_key * keep[:, None, None], value_rows, precision=highest)
    whole_weight, carry_state = weight_and_prior_state(out_weight.T, state, lambda back: lasts[back])
    order = jnp.arange(tok_rows, dtype=jnp.int32)
    allowed = ((order[:, None] >= order[None, :]) & (episode[:, None] == episode[None, :])).astype(
        jnp.float32
    )
    scores = jnp.einsum("thd,shd->hts", lifted_query, lifted_key, precision=highest)
    inside = jnp.einsum("hts,shd->thd", scores * allowed[None], value_rows, precision=highest)
    outside = jnp.einsum("thd,hde->the", lifted_query, carry_state, precision=highest)
    attn = inside + outside * (episode == prior).astype(jnp.float32)[:, None, None]
    mean_square = jnp.mean(attn * attn, axis=2, keepdims=True)
    scaled = attn * lax.rsqrt(mean_square + 1e-06) * attn_gain.reshape(heads_local, HEAD_DIM)
    headed = scaled.reshape(tok_rows, heads_local * HEAD_DIM).astype(jnp.bfloat16)

    x, core = lax.axis_index("x"), lax.axis_index("core")

    def mixed_for(headed, distance, same):
        target = ((x + distance) % 4) * 2 + (core if same else 1 - core)
        columns = lax.dynamic_index_in_dim(whole_weight, target, 0, keepdims=False)
        return lax.dot_general(headed, columns, (((1,), (1,)), ((), ())), preferred_element_type=jnp.float32)

    hidden = wide(residual) + summed_over_head(headed, mixed_for, False)
    scaled_rows = (hidden * norm_gain).astype(jnp.bfloat16)

    flat_ids = expert_ids.reshape(-1)
    pair_order = jnp.arange(flat_ids.shape[0])
    same = (flat_ids[:, None] == flat_ids[None, :]) & (pair_order[:, None] > pair_order[None, :])
    slot = jnp.sum(same.astype(jnp.int32), axis=1)
    place = (flat_ids * capacity + slot).reshape(tok_rows, 2)
    row_order = jnp.arange(rows, dtype=jnp.int32)
    chosen = (row_order[:, None] == place[:, 0][None, :]) | (row_order[:, None] == place[:, 1][None, :])
    outgoing = dot(chosen.astype(jnp.bfloat16), scaled_rows).astype(jnp.bfloat16)
    outgoing, late_gain = lax.optimization_barrier((outgoing, norm_gain))
    arrived = lax.all_to_all(
        outgoing.reshape(experts_count, capacity, features), CTX, split_axis=0, concat_axis=0, tiled=True
    ).reshape(rows, features)
    arrived, gains = lax.optimization_barrier((arrived, gathered_gains(late_gain)))

    near, far = rows_over_head(arrived)
    squared = lambda part, gain: jnp.sum(jnp.square(wide(part) / gain), axis=1, keepdims=True)
    gate_near, up_near, squares, far = lax.optimization_barrier(
        (dot(near, gate_weight[0]), dot(near, up_weight[0]), squared(near, gains), far)
    )
    far = jnp.concatenate(far)
    other = shift(far, "core", 1)
    far = jnp.where(core == 0, jnp.concatenate([far, other], 1), jnp.concatenate([other, far], 1))
    at_far = lambda value, dim: lax.dynamic_slice_in_dim(
        value, ((x + 2) % 4) * 2 * features, 2 * features, dim
    )
    squares = squares + squared(far, at_far(gains, 1))
    scale = lax.rsqrt(squares / near.shape[1] + 1e-06)
    gate = (gate_near + dot(far, at_far(gate_weight[0], 0))) * scale
    up = (up_near + dot(far, at_far(up_weight[0], 0))) * scale
    gated = narrow(jax.nn.silu(gate) * up)

    def part_of(partial, distance, same):
        target = ((x + distance) % 4) * 2 + (core if same else 1 - core)
        return lax.dynamic_slice_in_dim(partial, target * features, features, 1)

    partial = lax.optimization_barrier(narrow(dot(gated, down_weight[0])))
    summed = narrow(summed_over_head(partial, part_of, True))
    returned = lax.all_to_all(
        summed.reshape(experts_count, capacity, features), CTX, split_axis=0, concat_axis=0, tiled=True
    ).reshape(rows, features)

    raw_weights = route_weights.astype(jnp.float32)
    share = raw_weights / jnp.sum(raw_weights, axis=1, keepdims=True)
    spread = sum(
        jnp.where(place[:, k][:, None] == row_order[None, :], share[:, k][:, None], 0.0) for k in (0, 1)
    )
    coarse = lax.reduce_precision(spread, 8, 7)
    fine = (spread - coarse).astype(jnp.bfloat16)
    weighted = dot(coarse.astype(jnp.bfloat16), returned) + dot(fine, returned)
    return (hidden + weighted).astype(jnp.bfloat16)


def solution(mesh):
    torus = Mesh(mesh.devices.reshape(8, 4, 4, 2), (*CTX, *HEAD))
    in_specs = (
        P(CTX, HEAD),
        P(CTX, HEAD),
        P(CTX, HEAD),
        P(),
        P(HEAD),
        P(HEAD, CTX),
        P(CTX, HEAD),
        P(HEAD),
        P(CTX, None),
        P(CTX, None),
        P(CTX, None, HEAD),
        P(CTX, None, HEAD),
        P(CTX, HEAD, None),
    )
    return jax.shard_map(
        on_device, mesh=torus, in_specs=in_specs, out_specs=P(CTX, HEAD), check_vma=False
    )
```

```python
import jax
import jax.numpy as jnp
from jax import lax
from jax.sharding import Mesh
from jax.sharding import PartitionSpec as P

HEAD_DIM = 128
LONGEST = 4096
CTX = ("z", "y")
HEAD = ("x", "core")

highest = lax.Precision.HIGHEST


def shift(value, axis, step):
    size = lax.axis_size(axis)
    return lax.ppermute(value, axis, [(i, (i + step) % size) for i in range(size)])


def gathered_over_y(block):
    size, me = lax.axis_size("y"), lax.axis_index("y")
    return [(me, block)] + [((me - step) % size, shift(block, "y", step)) for step in (1, -1, 2)]


def laid_out(pieces, size):
    first = pieces[0][1]
    buffer = jnp.zeros((size, *first.shape), first.dtype)
    for index, piece in pieces:
        buffer = lax.dynamic_update_slice_in_dim(buffer, piece[None], index, 0)
    return buffer


def episode_of(positions, lengths):
    count = lengths.shape[0]
    ahead = jnp.arange(count)[:, None] > jnp.arange(count)[None, :]
    starts = jnp.sum(jnp.where(ahead, lengths[None, :], 0), axis=1)
    return jnp.sum((starts[None, :] <= positions[:, None]).astype(jnp.int32), axis=1) - 1


def weight_and_prior_state(weight, state, last):
    size, me = lax.axis_size("z"), lax.axis_index("z")
    goal = last(1)
    joined = lambda total, far, back: total + jnp.where(last(back) == goal, wide(far), 0.0)

    def after(value, *others):
        return lax.optimization_barrier((value, *others))[0]

    first = gathered_over_y(weight)
    sent = after(narrow(state), *(part for _, part in first))
    slab = laid_out(first, lax.axis_size("y")).reshape(-1, weight.shape[1])

    up, down = shift(slab, "z", 1), shift(slab, "z", -1)
    total = joined(joined(0.0, shift(sent, CTX, 1), 1), shift(sent, CTX, 2), 2)
    near = after(narrow(total), up, down)
    found = [(me, slab), ((me - 1) % size, up), ((me + 1) % size, down)]

    up, down = shift(up, "z", 1), shift(down, "z", -1)
    total = joined(total, shift(near, CTX, 2), 3)
    near = after(narrow(total), up, down)
    found += [((me - 2) % size, up), ((me + 2) % size, down)]

    up, down = shift(up, "z", 1), shift(down, "z", -1)
    total = joined(total, shift(near, CTX, 4), 5)
    near = after(narrow(total), up, down)
    found += [((me - 3) % size, up), ((me + 3) % size, down)]

    half = slab.shape[0] // 2
    opposite = jnp.concatenate([shift(up[:half], "z", 1), shift(down[half:], "z", -1)])
    total = joined(total, shift(near, CTX, 8), 9)
    found += [((me + 4) % size, opposite)]
    return laid_out(found, size), total


def halves(value):
    middle = value.shape[0] // 2
    return value[:middle], value[middle:]


def narrow(value):
    return value.astype(jnp.bfloat16)


def wide(value):
    return value.astype(jnp.float32)


def summed_over_head(source, part, in_halves):
    def pair(distance):
        return wide(part(source, distance, True)) + wide(shift(narrow(part(source, distance, False)), "core", 1))

    first = narrow(part(source, 2, False))
    first, source = lax.optimization_barrier((first, source))
    far = narrow(wide(part(source, 2, True)) + wide(shift(first, "core", 1)))
    if in_halves:
        far, source = lax.optimization_barrier((far, source))
    top, low = halves(far)
    above, below = shift(top, "x", 1), shift(low, "x", -1)
    up_top, up_low = halves(pair(1))
    down_top, down_low = halves(pair(3))
    if in_halves:
        up_low = shift(narrow(up_low), "x", 1)
        down_top = shift(narrow(down_top), "x", -1)
        up_top = shift(narrow(up_top + wide(above)), "x", 1)
        down_low = shift(narrow(down_low + wide(below)), "x", -1)
        top, low = halves(pair(0))
        return jnp.concatenate([top + wide(up_top) + wide(down_top), low + wide(up_low) + wide(down_low)])
    up = shift(jnp.concatenate([narrow(up_top + wide(above)), narrow(up_low)]), "x", 1)
    down = shift(jnp.concatenate([narrow(down_top), narrow(down_low + wide(below))]), "x", -1)
    return pair(0) + wide(up) + wide(down)


def gathered_gains(gain):
    x, core = lax.axis_index("x"), lax.axis_index("core")
    other = shift(gain, "core", 1)
    pair = jnp.where(core == 0, jnp.stack([gain, other]), jnp.stack([other, gain]))
    found = [((x - step) % 4, shift(pair, "x", step) if step else pair) for step in (0, 1, -1, 2)]
    return laid_out(found, 4).reshape(1, -1)


def rows_over_head(block):
    x, core = lax.axis_index("x"), lax.axis_index("core")
    rows, features = block.shape
    half = rows // 2
    from_low, from_high = shift(block, "x", 1), shift(block, "x", -1)
    far = (shift(from_low[:half], "x", 1), shift(from_high[half:], "x", -1))
    near = jnp.zeros((rows, features * 8), block.dtype)
    for source, part in ((x, block), ((x + 3) % 4, from_low), ((x + 1) % 4, from_high)):
        for place, piece in ((core, part), (1 - core, shift(part, "core", 1))):
            near = lax.dynamic_update_slice_in_dim(near, piece, (source * 2 + place) * features, 1)
    return near, far


def dot(a, b):
    return jnp.dot(a, b, preferred_element_type=jnp.float32)


def on_device(
    query,
    key,
    value,
    episode_lengths,
    attn_gain,
    out_weight,
    residual,
    norm_gain,
    expert_ids,
    route_weights,
    gate_weight,
    up_weight,
    down_weight,
):
    tok_rows = query.shape[0]
    heads_local = query.shape[1] // HEAD_DIM
    features = residual.shape[1]
    own_index = lax.axis_index(CTX)
    experts_count = gate_weight.shape[0] * lax.axis_size(CTX)
    capacity = 3 * tok_rows // experts_count
    rows = experts_count * capacity

    positions = own_index * tok_rows + jnp.arange(tok_rows, dtype=jnp.int32)
    episode = episode_of(positions, episode_lengths)
    lasts = episode_of((own_index + 1 - jnp.arange(LONGEST // tok_rows + 2, dtype=jnp.int32)) * tok_rows - 1, episode_lengths)
    final, prior = lasts[0], lasts[1]
    lifted_query = jax.nn.silu(query.astype(jnp.float32)).reshape(tok_rows, heads_local, HEAD_DIM)
    lifted_key = jax.nn.silu(key.astype(jnp.float32)).reshape(tok_rows, heads_local, HEAD_DIM)
    value_rows = value.astype(jnp.float32).reshape(tok_rows, heads_local, HEAD_DIM)
    keep = (episode == final).astype(jnp.float32)
    state = jnp.einsum("shd,she->hde", lifted_key * keep[:, None, None], value_rows, precision=highest)
    whole_weight, carry_state = weight_and_prior_state(out_weight.T, state, lambda back: lasts[back])
    order = jnp.arange(tok_rows, dtype=jnp.int32)
    allowed = ((order[:, None] >= order[None, :]) & (episode[:, None] == episode[None, :])).astype(
        jnp.float32
    )
    scores = jnp.einsum("thd,shd->hts", lifted_query, lifted_key, precision=highest)
    inside = jnp.einsum("hts,shd->thd", scores * allowed[None], value_rows, precision=highest)
    outside = jnp.einsum("thd,hde->the", lifted_query, carry_state, precision=highest)
    attn = inside + outside * (episode == prior).astype(jnp.float32)[:, None, None]
    mean_square = jnp.mean(attn * attn, axis=2, keepdims=True)
    scaled = attn * lax.rsqrt(mean_square + 1e-06) * attn_gain.reshape(heads_local, HEAD_DIM)
    headed = scaled.reshape(tok_rows, heads_local * HEAD_DIM).astype(jnp.bfloat16)

    x, core = lax.axis_index("x"), lax.axis_index("core")

    def mixed_for(headed, distance, same):
        target = ((x + distance) % 4) * 2 + (core if same else 1 - core)
        columns = lax.dynamic_index_in_dim(whole_weight, target, 0, keepdims=False)
        return lax.dot_general(headed, columns, (((1,), (1,)), ((), ())), preferred_element_type=jnp.float32)

    hidden = wide(residual) + summed_over_head(headed, mixed_for, False)
    scaled_rows = (hidden * norm_gain).astype(jnp.bfloat16)

    flat_ids = expert_ids.reshape(-1)
    pair_order = jnp.arange(flat_ids.shape[0])
    same = (flat_ids[:, None] == flat_ids[None, :]) & (pair_order[:, None] > pair_order[None, :])
    slot = jnp.sum(same.astype(jnp.int32), axis=1)
    place = (flat_ids * capacity + slot).reshape(tok_rows, 2)
    row_order = jnp.arange(rows, dtype=jnp.int32)
    chosen = (row_order[:, None] == place[:, 0][None, :]) | (row_order[:, None] == place[:, 1][None, :])
    outgoing = dot(chosen.astype(jnp.bfloat16), scaled_rows).astype(jnp.bfloat16)
    outgoing, late_gain = lax.optimization_barrier((outgoing, norm_gain))
    arrived = lax.all_to_all(
        outgoing.reshape(experts_count, capacity, features), CTX, split_axis=0, concat_axis=0, tiled=True
    ).reshape(rows, features)
    arrived, gains = lax.optimization_barrier((arrived, gathered_gains(late_gain)))

    near, far = rows_over_head(arrived)
    squared = lambda part, gain: jnp.sum(jnp.square(wide(part) / gain), axis=1, keepdims=True)
    gate_near, far = lax.optimization_barrier((dot(near, gate_weight[0]), far))
    far = jnp.concatenate(far)
    up_near, squares, other = lax.optimization_barrier(
        (dot(near, up_weight[0]), squared(near, gains), shift(far, "core", 1))
    )
    far = jnp.where(core == 0, jnp.concatenate([far, other], 1), jnp.concatenate([other, far], 1))
    at_far = lambda value, dim: lax.dynamic_slice_in_dim(
        value, ((x + 2) % 4) * 2 * features, 2 * features, dim
    )
    squares = squares + squared(far, at_far(gains, 1))
    scale = lax.rsqrt(squares / near.shape[1] + 1e-06)
    gate = (gate_near + dot(far, at_far(gate_weight[0], 0))) * scale
    up = (up_near + dot(far, at_far(up_weight[0], 0))) * scale
    gated = narrow(jax.nn.silu(gate) * up)

    def partial_for(gated, distance, same):
        target = ((x + distance) % 4) * 2 + (core if same else 1 - core)
        return dot(gated, lax.dynamic_slice_in_dim(down_weight[0], target * features, features, 1))

    summed = narrow(summed_over_head(lax.optimization_barrier(gated), partial_for, True))
    returned = lax.all_to_all(
        summed.reshape(experts_count, capacity, features), CTX, split_axis=0, concat_axis=0, tiled=True
    ).reshape(rows, features)

    raw_weights = route_weights.astype(jnp.float32)
    share = raw_weights / jnp.sum(raw_weights, axis=1, keepdims=True)
    spread = sum(
        jnp.where(place[:, k][:, None] == row_order[None, :], share[:, k][:, None], 0.0) for k in (0, 1)
    )
    coarse = lax.reduce_precision(spread, 8, 7)
    fine = (spread - coarse).astype(jnp.bfloat16)
    weighted = dot(coarse.astype(jnp.bfloat16), returned) + dot(fine, returned)
    return (hidden + weighted).astype(jnp.bfloat16)


def solution(mesh):
    torus = Mesh(mesh.devices.reshape(8, 4, 4, 2), (*CTX, *HEAD))
    in_specs = (
        P(CTX, HEAD),
        P(CTX, HEAD),
        P(CTX, HEAD),
        P(),
        P(HEAD),
        P(HEAD, CTX),
        P(CTX, HEAD),
        P(HEAD),
        P(CTX, None),
        P(CTX, None),
        P(CTX, None, HEAD),
        P(CTX, None, HEAD),
        P(CTX, HEAD, None),
    )
    return jax.shard_map(
        on_device, mesh=torus, in_specs=in_specs, out_specs=P(CTX, HEAD), check_vma=False
    )
```

```python
import jax
import jax.numpy as jnp
from jax import lax
from jax.sharding import Mesh
from jax.sharding import PartitionSpec as P

HEAD_DIM = 128
LONGEST = 4096
CTX = ("z", "y")
HEAD = ("x", "core")

highest = lax.Precision.HIGHEST


def shift(value, axis, step):
    size = lax.axis_size(axis)
    return lax.ppermute(value, axis, [(i, (i + step) % size) for i in range(size)])


def gathered_over_y(block):
    size, me = lax.axis_size("y"), lax.axis_index("y")
    return [(me, block)] + [((me - step) % size, shift(block, "y", step)) for step in (1, -1, 2)]


def laid_out(pieces, size):
    first = pieces[0][1]
    buffer = jnp.zeros((size, *first.shape), first.dtype)
    for index, piece in pieces:
        buffer = lax.dynamic_update_slice_in_dim(buffer, piece[None], index, 0)
    return buffer


def episode_of(positions, lengths):
    count = lengths.shape[0]
    ahead = jnp.arange(count)[:, None] > jnp.arange(count)[None, :]
    starts = jnp.sum(jnp.where(ahead, lengths[None, :], 0), axis=1)
    return jnp.sum((starts[None, :] <= positions[:, None]).astype(jnp.int32), axis=1) - 1


def after(value, *others):
    return lax.optimization_barrier((value, *others))[0]


def weight_and_prior_state(first, state, last):
    size, me = lax.axis_size("z"), lax.axis_index("z")
    goal = last(1)
    joined = lambda total, far, back: total + jnp.where(last(back) == goal, wide(far), 0.0)

    sent = narrow(state)
    slab = laid_out(first, lax.axis_size("y")).reshape(-1, first[0][1].shape[1])

    up, down = shift(slab, "z", 1), shift(slab, "z", -1)
    total = joined(joined(0.0, shift(sent, CTX, 1), 1), shift(sent, CTX, 2), 2)
    near = after(narrow(total), up, down)
    found = [(me, slab), ((me - 1) % size, up), ((me + 1) % size, down)]

    up, down = shift(up, "z", 1), shift(down, "z", -1)
    total = joined(total, shift(near, CTX, 2), 3)
    near = after(narrow(total), up, down)
    found += [((me - 2) % size, up), ((me + 2) % size, down)]

    up, down = shift(up, "z", 1), shift(down, "z", -1)
    total = joined(total, shift(near, CTX, 4), 5)
    near = after(narrow(total), up, down)
    found += [((me - 3) % size, up), ((me + 3) % size, down)]

    half = slab.shape[0] // 2
    opposite = jnp.concatenate([shift(up[:half], "z", 1), shift(down[half:], "z", -1)])
    total = joined(total, shift(near, CTX, 8), 9)
    found += [((me + 4) % size, opposite)]
    return laid_out(found, size), total


def halves(value):
    middle = value.shape[0] // 2
    return value[:middle], value[middle:]


def narrow(value):
    return value.astype(jnp.bfloat16)


def wide(value):
    return value.astype(jnp.float32)


def summed_over_head(source, part, in_halves):
    def pair(distance):
        return wide(part(source, distance, True)) + wide(shift(narrow(part(source, distance, False)), "core", 1))

    first = narrow(part(source, 2, False))
    first, source = lax.optimization_barrier((first, source))
    far = narrow(wide(part(source, 2, True)) + wide(shift(first, "core", 1)))
    if in_halves:
        far, source = lax.optimization_barrier((far, source))
    top, low = halves(far)
    above, below = shift(top, "x", 1), shift(low, "x", -1)
    up_top, up_low = halves(pair(1))
    down_top, down_low = halves(pair(3))
    if in_halves:
        up_low = shift(narrow(up_low), "x", 1)
        down_top = shift(narrow(down_top), "x", -1)
        up_top = shift(narrow(up_top + wide(above)), "x", 1)
        down_low = shift(narrow(down_low + wide(below)), "x", -1)
        top, low = halves(pair(0))
        top, low = lax.optimization_barrier((top + wide(down_top), low + wide(up_low)))
        return jnp.concatenate([top + wide(up_top), low + wide(down_low)])
    up = shift(jnp.concatenate([narrow(up_top + wide(above)), narrow(up_low)]), "x", 1)
    down = shift(jnp.concatenate([narrow(down_top), narrow(down_low + wide(below))]), "x", -1)
    return pair(0) + wide(up) + wide(down)


def gathered_gains(gain):
    x, core = lax.axis_index("x"), lax.axis_index("core")
    other = shift(gain, "core", 1)
    pair = jnp.where(core == 0, jnp.stack([gain, other]), jnp.stack([other, gain]))
    found = [((x - step) % 4, shift(pair, "x", step) if step else pair) for step in (0, 1, -1, 2)]
    return laid_out(found, 4).reshape(1, -1)


def rows_over_head(block):
    x, core = lax.axis_index("x"), lax.axis_index("core")
    rows, features = block.shape
    half = rows // 2
    from_low, from_high = shift(block, "x", 1), shift(block, "x", -1)
    far = (shift(from_low[:half], "x", 1), shift(from_high[half:], "x", -1))
    near = jnp.zeros((rows, features * 8), block.dtype)
    for source, part in ((x, block), ((x + 3) % 4, from_low), ((x + 1) % 4, from_high)):
        for place, piece in ((core, part), (1 - core, shift(part, "core", 1))):
            near = lax.dynamic_update_slice_in_dim(near, piece, (source * 2 + place) * features, 1)
    return near, far


def dot(a, b):
    return jnp.dot(a, b, preferred_element_type=jnp.float32)


def on_device(
    query,
    key,
    value,
    episode_lengths,
    attn_gain,
    out_weight,
    residual,
    norm_gain,
    expert_ids,
    route_weights,
    gate_weight,
    up_weight,
    down_weight,
):
    tok_rows = query.shape[0]
    heads_local = query.shape[1] // HEAD_DIM
    features = residual.shape[1]
    own_index = lax.axis_index(CTX)
    experts_count = gate_weight.shape[0] * lax.axis_size(CTX)
    capacity = 3 * tok_rows // experts_count
    rows = experts_count * capacity

    weight_by_y = gathered_over_y(out_weight.T)
    key = after(key, *(part for _, part in weight_by_y))
    positions = own_index * tok_rows + jnp.arange(tok_rows, dtype=jnp.int32)
    episode = episode_of(positions, episode_lengths)
    lasts = episode_of((own_index + 1 - jnp.arange(LONGEST // tok_rows + 2, dtype=jnp.int32)) * tok_rows - 1, episode_lengths)
    final, prior = lasts[0], lasts[1]
    lifted_query = jax.nn.silu(query.astype(jnp.float32)).reshape(tok_rows, heads_local, HEAD_DIM)
    lifted_key = jax.nn.silu(key.astype(jnp.float32)).reshape(tok_rows, heads_local, HEAD_DIM)
    value_rows = value.astype(jnp.float32).reshape(tok_rows, heads_local, HEAD_DIM)
    keep = (episode == final).astype(jnp.float32)
    state = jnp.einsum("shd,she->hde", lifted_key * keep[:, None, None], value_rows, precision=highest)
    whole_weight, carry_state = weight_and_prior_state(weight_by_y, state, lambda back: lasts[back])
    order = jnp.arange(tok_rows, dtype=jnp.int32)
    allowed = ((order[:, None] >= order[None, :]) & (episode[:, None] == episode[None, :])).astype(
        jnp.float32
    )
    scores = jnp.einsum("thd,shd->hts", lifted_query, lifted_key, precision=highest)
    inside = jnp.einsum("hts,shd->thd", scores * allowed[None], value_rows, precision=highest)
    outside = jnp.einsum("thd,hde->the", lifted_query, carry_state, precision=highest)
    attn = inside + outside * (episode == prior).astype(jnp.float32)[:, None, None]
    mean_square = jnp.mean(attn * attn, axis=2, keepdims=True)
    scaled = attn * lax.rsqrt(mean_square + 1e-06) * attn_gain.reshape(heads_local, HEAD_DIM)
    headed = scaled.reshape(tok_rows, heads_local * HEAD_DIM).astype(jnp.bfloat16)

    x, core = lax.axis_index("x"), lax.axis_index("core")

    def mixed_for(headed, distance, same):
        target = ((x + distance) % 4) * 2 + (core if same else 1 - core)
        columns = lax.dynamic_index_in_dim(whole_weight, target, 0, keepdims=False)
        return lax.dot_general(headed, columns, (((1,), (1,)), ((), ())), preferred_element_type=jnp.float32)

    hidden = wide(residual) + summed_over_head(headed, mixed_for, False)
    scaled_rows = (hidden * norm_gain).astype(jnp.bfloat16)

    flat_ids = expert_ids.reshape(-1)
    pair_order = jnp.arange(flat_ids.shape[0])
    same = (flat_ids[:, None] == flat_ids[None, :]) & (pair_order[:, None] > pair_order[None, :])
    slot = jnp.sum(same.astype(jnp.int32), axis=1)
    place = (flat_ids * capacity + slot).reshape(tok_rows, 2)
    row_order = jnp.arange(rows, dtype=jnp.int32)
    chosen = (row_order[:, None] == place[:, 0][None, :]) | (row_order[:, None] == place[:, 1][None, :])
    outgoing = dot(chosen.astype(jnp.bfloat16), scaled_rows).astype(jnp.bfloat16)
    outgoing, late_gain = lax.optimization_barrier((outgoing, norm_gain))
    arrived = lax.all_to_all(
        outgoing.reshape(experts_count, capacity, features), CTX, split_axis=0, concat_axis=0, tiled=True
    ).reshape(rows, features)
    arrived, gains = lax.optimization_barrier((arrived, gathered_gains(late_gain)))

    near, far = rows_over_head(arrived)
    squared = lambda part, gain: jnp.sum(jnp.square(wide(part) / gain), axis=1, keepdims=True)
    gate_near, far = lax.optimization_barrier((dot(near, gate_weight[0]), far))
    far = jnp.concatenate(far)
    up_near, squares, other = lax.optimization_barrier(
        (dot(near, up_weight[0]), squared(near, gains), shift(far, "core", 1))
    )
    far = jnp.where(core == 0, jnp.concatenate([far, other], 1), jnp.concatenate([other, far], 1))
    at_far = lambda value, dim: lax.dynamic_slice_in_dim(
        value, ((x + 2) % 4) * 2 * features, 2 * features, dim
    )
    squares = squares + squared(far, at_far(gains, 1))
    scale = lax.rsqrt(squares / near.shape[1] + 1e-06)
    gate = (gate_near + dot(far, at_far(gate_weight[0], 0))) * scale
    up = (up_near + dot(far, at_far(up_weight[0], 0))) * scale
    gated = narrow(jax.nn.silu(gate) * up)

    def partial_for(gated, distance, same):
        target = ((x + distance) % 4) * 2 + (core if same else 1 - core)
        return dot(gated, lax.dynamic_slice_in_dim(down_weight[0], target * features, features, 1))

    summed = narrow(summed_over_head(lax.optimization_barrier(gated), partial_for, True))
    returned = lax.all_to_all(
        summed.reshape(experts_count, capacity, features), CTX, split_axis=0, concat_axis=0, tiled=True
    ).reshape(rows, features)

    raw_weights = route_weights.astype(jnp.float32)
    share = raw_weights / jnp.sum(raw_weights, axis=1, keepdims=True)
    spread = sum(
        jnp.where(place[:, k][:, None] == row_order[None, :], share[:, k][:, None], 0.0) for k in (0, 1)
    )
    coarse = lax.reduce_precision(spread, 8, 7)
    fine = (spread - coarse).astype(jnp.bfloat16)
    weighted = dot(coarse.astype(jnp.bfloat16), returned) + dot(fine, returned)
    return (hidden + weighted).astype(jnp.bfloat16)


def solution(mesh):
    torus = Mesh(mesh.devices.reshape(8, 4, 4, 2), (*CTX, *HEAD))
    in_specs = (
        P(CTX, HEAD),
        P(CTX, HEAD),
        P(CTX, HEAD),
        P(),
        P(HEAD),
        P(HEAD, CTX),
        P(CTX, HEAD),
        P(HEAD),
        P(CTX, None),
        P(CTX, None),
        P(CTX, None, HEAD),
        P(CTX, None, HEAD),
        P(CTX, HEAD, None),
    )
    return jax.shard_map(
        on_device, mesh=torus, in_specs=in_specs, out_specs=P(CTX, HEAD), check_vma=False
    )
```

```python
import jax
import jax.numpy as jnp
from jax import lax
from jax.sharding import Mesh
from jax.sharding import PartitionSpec as P

HEAD_DIM = 128
LONGEST = 4096
CTX = ("z", "y")
HEAD = ("x", "core")

highest = lax.Precision.HIGHEST


def shift(value, axis, step):
    size = lax.axis_size(axis)
    return lax.ppermute(value, axis, [(i, (i + step) % size) for i in range(size)])


def gathered_over_y(block):
    size, me = lax.axis_size("y"), lax.axis_index("y")
    return [(me, block)] + [((me - step) & (size - 1), shift(block, "y", step)) for step in (1, -1, 2)]


def laid_out(pieces, size):
    first = pieces[0][1]
    buffer = jnp.zeros((size, *first.shape), first.dtype)
    for index, piece in pieces:
        buffer = lax.dynamic_update_slice_in_dim(buffer, piece[None], index, 0)
    return buffer


def episode_of(positions, lengths):
    count = lengths.shape[0]
    ahead = jnp.arange(count)[:, None] > jnp.arange(count)[None, :]
    starts = jnp.sum(jnp.where(ahead, lengths[None, :], 0), axis=1)
    return jnp.sum((starts[None, :] <= positions[:, None]).astype(jnp.int32), axis=1) - 1


def after(value, *others):
    return lax.optimization_barrier((value, *others))[0]


def weight_and_prior_state(first, state, last):
    size, me = lax.axis_size("z"), lax.axis_index("z")
    goal = last(1)
    joined = lambda total, far, back: total + jnp.where(last(back) == goal, wide(far), 0.0)

    sent = narrow(state)
    slab = laid_out(first, lax.axis_size("y")).reshape(-1, first[0][1].shape[1])

    up, down = shift(slab, "z", 1), shift(slab, "z", -1)
    total = joined(joined(0.0, shift(sent, CTX, 1), 1), shift(sent, CTX, 2), 2)
    near = after(narrow(total), up, down)
    found = [(me, slab), ((me - 1) & (size - 1), up), ((me + 1) & (size - 1), down)]

    up, down = shift(up, "z", 1), shift(down, "z", -1)
    total = joined(total, shift(near, CTX, 2), 3)
    near = after(narrow(total), up, down)
    found += [((me - 2) & (size - 1), up), ((me + 2) & (size - 1), down)]

    up, down = shift(up, "z", 1), shift(down, "z", -1)
    total = joined(total, shift(near, CTX, 4), 5)
    near = after(narrow(total), up, down)
    found += [((me - 3) & (size - 1), up), ((me + 3) & (size - 1), down)]

    half = slab.shape[0] // 2
    opposite = jnp.concatenate([shift(up[:half], "z", 1), shift(down[half:], "z", -1)])
    total = joined(total, shift(near, CTX, 8), 9)
    found += [((me + 4) & (size - 1), opposite)]
    return laid_out(found, size), total


def halves(value):
    middle = value.shape[0] // 2
    return value[:middle], value[middle:]


def narrow(value):
    return value.astype(jnp.bfloat16)


def wide(value):
    return value.astype(jnp.float32)


def summed_over_head(source, part, in_halves):
    def pair(distance):
        return wide(part(source, distance, True)) + wide(shift(narrow(part(source, distance, False)), "core", 1))

    first = narrow(part(source, 2, False))
    first, source = lax.optimization_barrier((first, source))
    far = narrow(wide(part(source, 2, True)) + wide(shift(first, "core", 1)))
    if in_halves:
        far, source = lax.optimization_barrier((far, source))
    top, low = halves(far)
    above, below = shift(top, "x", 1), shift(low, "x", -1)
    up_top, up_low = halves(pair(1))
    down_top, down_low = halves(pair(3))
    if in_halves:
        up_low = shift(narrow(up_low), "x", 1)
        down_top = shift(narrow(down_top), "x", -1)
        up_top = shift(narrow(up_top + wide(above)), "x", 1)
        down_low = shift(narrow(down_low + wide(below)), "x", -1)
        top, low = halves(pair(0))
        top, low = lax.optimization_barrier((top + wide(down_top), low + wide(up_low)))
        return jnp.concatenate([top + wide(up_top), low + wide(down_low)])
    up = shift(jnp.concatenate([narrow(up_top + wide(above)), narrow(up_low)]), "x", 1)
    down = shift(jnp.concatenate([narrow(down_top), narrow(down_low + wide(below))]), "x", -1)
    return pair(0) + wide(up) + wide(down)


def gathered_gains(gain):
    x, core = lax.axis_index("x"), lax.axis_index("core")
    other = shift(gain, "core", 1)
    pair = jnp.where(core == 0, jnp.stack([gain, other]), jnp.stack([other, gain]))
    found = [((x - step) & 3, shift(pair, "x", step) if step else pair) for step in (0, 1, -1, 2)]
    return laid_out(found, 4).reshape(1, -1)


def rows_over_head(block):
    x, core = lax.axis_index("x"), lax.axis_index("core")
    rows, features = block.shape
    half = rows // 2
    from_low, from_high = shift(block, "x", 1), shift(block, "x", -1)
    far = (shift(from_low[:half], "x", 1), shift(from_high[half:], "x", -1))
    near = jnp.zeros((rows, features * 8), block.dtype)
    for source, part in ((x, block), ((x + 3) & 3, from_low), ((x + 1) & 3, from_high)):
        for place, piece in ((core, part), (1 - core, shift(part, "core", 1))):
            near = lax.dynamic_update_slice_in_dim(near, piece, (source * 2 + place) * features, 1)
    return near, far


def dot(a, b):
    return jnp.dot(a, b, preferred_element_type=jnp.float32)


def on_device(
    query,
    key,
    value,
    episode_lengths,
    attn_gain,
    out_weight,
    residual,
    norm_gain,
    expert_ids,
    route_weights,
    gate_weight,
    up_weight,
    down_weight,
):
    tok_rows = query.shape[0]
    heads_local = query.shape[1] // HEAD_DIM
    features = residual.shape[1]
    own_index = lax.axis_index(CTX)
    experts_count = gate_weight.shape[0] * lax.axis_size(CTX)
    capacity = 3 * tok_rows // experts_count
    rows = experts_count * capacity

    weight_by_y = gathered_over_y(out_weight.T)
    key = after(key, *(part for _, part in weight_by_y))
    positions = own_index * tok_rows + jnp.arange(tok_rows, dtype=jnp.int32)
    episode = episode_of(positions, episode_lengths)
    lasts = episode_of((own_index + 1 - jnp.arange(LONGEST // tok_rows + 2, dtype=jnp.int32)) * tok_rows - 1, episode_lengths)
    final, prior = lasts[0], lasts[1]
    lifted_query = jax.nn.silu(query.astype(jnp.float32)).reshape(tok_rows, heads_local, HEAD_DIM)
    lifted_key = jax.nn.silu(key.astype(jnp.float32)).reshape(tok_rows, heads_local, HEAD_DIM)
    value_rows = value.astype(jnp.float32).reshape(tok_rows, heads_local, HEAD_DIM)
    keep = (episode == final).astype(jnp.float32)
    state = jnp.einsum("shd,she->hde", lifted_key * keep[:, None, None], value_rows, precision=highest)
    whole_weight, carry_state = weight_and_prior_state(weight_by_y, state, lambda back: lasts[back])
    order = jnp.arange(tok_rows, dtype=jnp.int32)
    allowed = ((order[:, None] >= order[None, :]) & (episode[:, None] == episode[None, :])).astype(
        jnp.float32
    )
    scores = jnp.einsum("thd,shd->hts", lifted_query, lifted_key, precision=highest)
    inside = jnp.einsum("hts,shd->thd", scores * allowed[None], value_rows, precision=highest)
    outside = jnp.einsum("thd,hde->the", lifted_query, carry_state, precision=highest)
    attn = inside + outside * (episode == prior).astype(jnp.float32)[:, None, None]
    mean_square = jnp.mean(attn * attn, axis=2, keepdims=True)
    scaled = attn * lax.rsqrt(mean_square + 1e-06) * attn_gain.reshape(heads_local, HEAD_DIM)
    headed = scaled.reshape(tok_rows, heads_local * HEAD_DIM).astype(jnp.bfloat16)

    x, core = lax.axis_index("x"), lax.axis_index("core")

    def mixed_for(headed, distance, same):
        target = ((x + distance) & 3) * 2 + (core if same else 1 - core)
        columns = lax.dynamic_index_in_dim(whole_weight, target, 0, keepdims=False)
        return lax.dot_general(headed, columns, (((1,), (1,)), ((), ())), preferred_element_type=jnp.float32)

    hidden = wide(residual) + summed_over_head(headed, mixed_for, False)
    scaled_rows = (hidden * norm_gain).astype(jnp.bfloat16)

    flat_ids = expert_ids.reshape(-1)
    pair_order = jnp.arange(flat_ids.shape[0])
    same = (flat_ids[:, None] == flat_ids[None, :]) & (pair_order[:, None] > pair_order[None, :])
    slot = jnp.sum(same.astype(jnp.int32), axis=1)
    place = (flat_ids * capacity + slot).reshape(tok_rows, 2)
    row_order = jnp.arange(rows, dtype=jnp.int32)
    chosen = (row_order[:, None] == place[:, 0][None, :]) | (row_order[:, None] == place[:, 1][None, :])
    outgoing = dot(chosen.astype(jnp.bfloat16), scaled_rows).astype(jnp.bfloat16)
    outgoing, late_gain = lax.optimization_barrier((outgoing, norm_gain))
    arrived = lax.all_to_all(
        outgoing.reshape(experts_count, capacity, features), CTX, split_axis=0, concat_axis=0, tiled=True
    ).reshape(rows, features)
    arrived, gains = lax.optimization_barrier((arrived, gathered_gains(late_gain)))

    near, far = rows_over_head(arrived)
    squared = lambda part, gain: jnp.sum(jnp.square(wide(part) / gain), axis=1, keepdims=True)
    gate_near, far = lax.optimization_barrier((dot(near, gate_weight[0]), far))
    far = jnp.concatenate(far)
    up_near, squares, other = lax.optimization_barrier(
        (dot(near, up_weight[0]), squared(near, gains), shift(far, "core", 1))
    )
    far = jnp.where(core == 0, jnp.concatenate([far, other], 1), jnp.concatenate([other, far], 1))
    at_far = lambda value, dim: lax.dynamic_slice_in_dim(
        value, ((x + 2) & 3) * 2 * features, 2 * features, dim
    )
    squares = squares + squared(far, at_far(gains, 1))
    scale = lax.rsqrt(squares / near.shape[1] + 1e-06)
    gate = (gate_near + dot(far, at_far(gate_weight[0], 0))) * scale
    up = (up_near + dot(far, at_far(up_weight[0], 0))) * scale
    gated = narrow(jax.nn.silu(gate) * up)

    def partial_for(gated, distance, same):
        target = ((x + distance) & 3) * 2 + (core if same else 1 - core)
        return dot(gated, lax.dynamic_slice_in_dim(down_weight[0], target * features, features, 1))

    summed = narrow(summed_over_head(lax.optimization_barrier(gated), partial_for, True))
    returned = lax.all_to_all(
        summed.reshape(experts_count, capacity, features), CTX, split_axis=0, concat_axis=0, tiled=True
    ).reshape(rows, features)

    raw_weights = route_weights.astype(jnp.float32)
    share = raw_weights / jnp.sum(raw_weights, axis=1, keepdims=True)
    spread = sum(
        jnp.where(place[:, k][:, None] == row_order[None, :], share[:, k][:, None], 0.0) for k in (0, 1)
    )
    coarse = lax.reduce_precision(spread, 8, 7)
    fine = (spread - coarse).astype(jnp.bfloat16)
    weighted = dot(coarse.astype(jnp.bfloat16), returned) + dot(fine, returned)
    return (hidden + weighted).astype(jnp.bfloat16)


def solution(mesh):
    torus = Mesh(mesh.devices.reshape(8, 4, 4, 2), (*CTX, *HEAD))
    in_specs = (
        P(CTX, HEAD),
        P(CTX, HEAD),
        P(CTX, HEAD),
        P(),
        P(HEAD),
        P(HEAD, CTX),
        P(CTX, HEAD),
        P(HEAD),
        P(CTX, None),
        P(CTX, None),
        P(CTX, None, HEAD),
        P(CTX, None, HEAD),
        P(CTX, HEAD, None),
    )
    return jax.shard_map(
        on_device, mesh=torus, in_specs=in_specs, out_specs=P(CTX, HEAD), check_vma=False
    )
```
